32 devices in a mesh: sec: 2 (over core), dom: 16 (over z, y, x).
Axes of the slice: x: 2, y: 2, z: 4, core: 2. Of those that a mesh axis runs over, the one named last changes fastest.
Arguments:
- state: float32 [3, 8, 262144], P(None, None, ('sec', 'dom')), may hold values from -6 to 6
- send_rows: int32 [524288], P(('sec', 'dom')), may hold values from 0 to 8191, as said below
- intersection_source: int32 [524288], P(('sec', 'dom')), may hold values from 0 to 16383, as said below
- intersection_weight: float32 [524288], P(('sec', 'dom')), may hold values from 0.1 to 1
- couple_rate: float32 [2, 3], P('sec'), may hold values from 0.2 to 0.8
- atm_metric: float32 [2, 131072], P(None, 'dom'), may hold values from 0.5 to 2
- wave_speed: float32 [8], replicated, may hold values from 0.5 to 2
- ocean_adjacent: int32 [6, 131072], P(None, 'dom'), may hold values from 0 to 9215, as said below
- ocean_edges: int32 [2, 8192], P(None, 'dom'), may hold values from 0 to 8191, as said below
- ocean_kappa: float32 [131072], P('dom'), may hold values from 0.02 to 0.15
Outputs:
- new_state: float32 [3, 8, 262144], P(None, None, ('sec', 'dom'))
The draws below stay inside these ranges and needn't reach their ends.
Inputs may be any that keep to these rules, and one draw needn't show every extreme that they name: `send_rows`: the ocean's band runs across the atmosphere's, so every block intersects every block of the other section. Within a block, cut the rows into 16 strips of 512 rows by position across the band; the 1024 slots for peer p hold the rows of strips p, p + 1, ... (modulo 16), 2 strips in all, in an order drawn from the seed; so every row fills exactly 2 slots. `intersection_source`: in each block a permutation of all 16384 received slots; the entries 2 * r .. 2 * r + 1 belong to row r. `ocean_adjacent`: each cell's neighbours on a hexagonal grid in its block's own row order; values from 8192 on name rim slots (first the cells of the previous block's last column, then those of the next block's first column, by position across the band); a cell at the band's edge names itself for a missing neighbour. `ocean_edges`: ordered by position across the band.
All inputs are finite; a program needn't handle non-finite values.
Results may differ from the reference program's by a relative error of at most 0.0001.
Values sent between devices are 32-bit elements; how exact they have to be, the bound alone decides.
A program may use at most 128 MiB of HBM per device.

```python
import math
import jax
import jax.numpy as jnp
import numpy as np
from jax import lax

LEV = 8
INTERSECTIONS = 2
XP = 16
YP = 512
ROWS = 8192
SLOTS = 16384
CAP = 1024
N_DOM = 16


def ocean_layout(key):
    base = jax.random.fold_in(key, 11)

    def one_device(device):
        order = jax.random.permutation(jax.random.fold_in(base, device), ROWS).astype(jnp.int32)
        places = jnp.zeros(ROWS, jnp.int32).at[order].set(jnp.arange(ROWS, dtype=jnp.int32))
        cells = jnp.arange(ROWS, dtype=jnp.int32)
        column = cells // YP
        height = cells % YP
        tilt = jnp.where(column % 2 == 1, 1, -1).astype(jnp.int32)
        zero_shift = jnp.zeros_like(cells)
        moves_x = [zero_shift, zero_shift, zero_shift + 1, zero_shift - 1, zero_shift + 1, zero_shift - 1]
        moves_y = [zero_shift + 1, zero_shift - 1, zero_shift, zero_shift, tilt, tilt]
        targets = []
        for moved_x, moved_y in zip(moves_x, moves_y):
            new_x = column + moved_x
            new_y = height + moved_y
            inside = (new_y >= 0) & (new_y < YP)
            safe_y = jnp.clip(new_y, 0, YP - 1)
            safe_x = jnp.clip(new_x, 0, XP - 1)
            local_row = places[safe_x * YP + safe_y]
            target = jnp.where(new_x < 0, ROWS + safe_y, jnp.where(new_x >= XP, ROWS + YP + safe_y, local_row))
            target = jnp.where(inside, target, places[cells])
            targets.append(target[order])
        positions = jnp.arange(YP, dtype=jnp.int32)
        edges = jnp.stack([places[positions], places[(XP - 1) * YP + positions]])
        return (jnp.stack(targets).astype(jnp.int32), edges.astype(jnp.int32), places)
    adjacency, edges, places = jax.vmap(one_device)(jnp.arange(N_DOM, dtype=jnp.int32))
    return (adjacency, edges, places)


def draw_ocean_adjacent(key, part):
    adjacency, edges, places = ocean_layout(key)
    return jnp.transpose(adjacency, (1, 0, 2)).reshape(6, N_DOM * ROWS)


def draw_ocean_edges(key, part):
    adjacency, edges, places = ocean_layout(key)
    return jnp.transpose(edges, (1, 0, 2)).reshape(2, N_DOM * YP)


def draw_send_rows(key, part):
    adjacency, edges, places = ocean_layout(key)
    base = jax.random.fold_in(key, 7)
    strip = ROWS // N_DOM
    order_ids = jnp.arange(ROWS, dtype=jnp.int32)
    crossing = order_ids % XP * YP + order_ids // XP

    def one_block(number):
        block_key = jax.random.fold_in(base, number)
        device = number % N_DOM
        lookup = jnp.where(number >= N_DOM, places[device], order_ids)
        listed = lookup[crossing]

        def one_peer(peer):
            shuffle = jax.random.permutation(jax.random.fold_in(block_key, peer), CAP).astype(jnp.int32)
            which = (peer + shuffle // strip) % N_DOM
            return listed[which * strip + shuffle % strip]
        return jax.vmap(one_peer)(jnp.arange(N_DOM, dtype=jnp.int32)).reshape(-1)
    return jax.vmap(one_block)(jnp.arange(2 * N_DOM, dtype=jnp.int32)).reshape(-1).astype(jnp.int32)


def draw_intersection_source(key, part):
    base = jax.random.fold_in(key, 5)

    def one_block(number):
        return jax.random.permutation(jax.random.fold_in(base, number), SLOTS).astype(jnp.int32)
    return jax.vmap(one_block)(jnp.arange(2 * N_DOM, dtype=jnp.int32)).reshape(-1)


def levels(stream_key, dims, pieces, least, top_value):
    loudness, own = 1.0, jax.random.fold_in(stream_key, 6)
    for dim, shards_of in pieces:
        draws = jnp.exp(jax.random.uniform(jax.random.fold_in(own, dim), (shards_of,), jnp.float32, least / len(pieces), top_value / len(pieces)))
        loudness = loudness * jnp.repeat(draws, dims[dim] // shards_of).reshape([-1 if axis == dim else 1 for axis in range(len(dims))])
    return loudness


def scatter_about(own_key, extent, scale, bound, split=(), kind=jnp.bfloat16):
    loudness = levels(own_key, extent, split, -0.22, 0.18) if split else 1.0
    values = jax.random.normal(own_key, extent, jnp.float32) * scale * loudness
    return jnp.minimum(jnp.maximum(values, -bound), bound).astype(kind)


def setup_inputs(seed: int = 0) -> dict:
    keys = jax.random.split(jax.random.key(seed), 11)
    return {
        "state": scatter_about(keys[0], (3, LEV, 2 * N_DOM * ROWS), 1.0, 6.0, ((2, 32),), jnp.float32),
        "send_rows": draw_send_rows(jax.random.fold_in(keys[10], 71), 0),
        "intersection_source": draw_intersection_source(jax.random.fold_in(keys[10], 71), 0),
        "intersection_weight": jnp.clip(jnp.exp(math.log(1.0) - 2.3025851 * jax.random.uniform(keys[3], (2 * N_DOM * INTERSECTIONS * ROWS,), jnp.float32) ** levels(keys[3], (2 * N_DOM * INTERSECTIONS * ROWS,), ((0, 32),), -0.2, 0.2)), 0.1, 1.0),
        "couple_rate": jnp.clip(0.2 + 0.6 * jax.random.uniform(keys[4], (2, 3), jnp.float32) ** levels(keys[4], (2, 3), ((0, 2),), -0.2, 0.2), 0.2, 0.8),
        "atm_metric": jnp.clip(jnp.exp(math.log(2.0) - 1.3862944 * jax.random.uniform(keys[5], (2, N_DOM * ROWS), jnp.float32) ** levels(keys[5], (2, N_DOM * ROWS), ((1, 16),), -0.2, 0.2)), 0.5, 2.0),
        "wave_speed": jnp.clip(jnp.exp(jax.random.uniform(keys[6], (LEV,), jnp.float32, math.log(0.5), math.log(2.0))), 0.5, 2.0),
        "ocean_adjacent": draw_ocean_adjacent(jax.random.fold_in(keys[10], 71), 0),
        "ocean_edges": draw_ocean_edges(jax.random.fold_in(keys[10], 71), 0),
        "ocean_kappa": jnp.clip(jnp.exp(math.log(0.15) - 2.014903 * jax.random.uniform(keys[9], (N_DOM * ROWS,), jnp.float32) ** levels(keys[9], (N_DOM * ROWS,), ((0, 16),), -0.2, 0.2)), 0.02, 0.15),
    }


TIME_STEP = 0.05

def gll_derivative():
    nodes = np.array([-1.0, -1.0 / np.sqrt(5.0), 1.0 / np.sqrt(5.0), 1.0])
    barycentric = np.array([1.0 / np.prod([nodes[first] - nodes[second] for second in range(4) if second != first]) for first in range(4)])
    matrix = np.zeros((4, 4))
    for first in range(4):
        for second in range(4):
            if first != second:
                matrix[first, second] = barycentric[second] / barycentric[first] / (nodes[first] - nodes[second])
        matrix[first, first] = -np.sum(matrix[first])
    return jnp.asarray(matrix, jnp.float32)

def along_first(field, derivative):
    depth, across, along = field.shape
    grouped = field.reshape(depth, across // 4, 4, along)
    return jnp.einsum('ij,lejy->leiy', derivative, grouped, precision=lax.Precision.HIGHEST).reshape(field.shape)

def along_second(field, derivative):
    depth, across, along = field.shape
    grouped = field.reshape(depth, across, along // 4, 4)
    return jnp.einsum('ij,lxej->lxei', derivative, grouped, precision=lax.Precision.HIGHEST).reshape(field.shape)

def dycore(fields, metric_x, metric_y, speeds):
    derivative = gll_derivative()
    eastward, northward, geopotential = (fields[0], fields[1], fields[2])
    slope_x = metric_x * along_first(geopotential, derivative)
    slope_y = metric_y * along_second(geopotential, derivative)
    spread = metric_x * along_first(eastward, derivative) + metric_y * along_second(northward, derivative)
    return jnp.stack([eastward - TIME_STEP * slope_x, northward - TIME_STEP * slope_y, geopotential - TIME_STEP * speeds[:, None, None] * spread])

def average_first(fields, before, after):
    phase = (jnp.arange(fields.shape[2]) % 4)[:, None]
    return jnp.where(phase == 3, (fields + after) * 0.5, jnp.where(phase == 0, (fields + before) * 0.5, fields))

def average_second(fields):
    along = fields.shape[3]
    position = jnp.arange(along)
    phase = position % 4
    after = jnp.roll(fields, -1, axis=3)
    before = jnp.roll(fields, 1, axis=3)
    joined_after = (phase == 3) & (position < along - 1)
    joined_before = (phase == 0) & (position > 0)
    return jnp.where(joined_after, (fields + after) * 0.5, jnp.where(joined_before, (fields + before) * 0.5, fields))

def reference(state, send_rows, intersection_source, intersection_weight, couple_rate, atm_metric, wave_speed, ocean_adjacent, ocean_edges, ocean_kappa):
    blocks = state.reshape(3, LEV, 2, N_DOM, ROWS)
    surface = blocks[:, LEV - 1]
    sender_rows = jnp.broadcast_to(send_rows.reshape(1, 2, N_DOM, SLOTS), (3, 2, N_DOM, SLOTS))
    outgoing = jnp.take_along_axis(surface, sender_rows, axis=3).reshape(3, 2, N_DOM, N_DOM, CAP)
    incoming = jnp.flip(outgoing, axis=1).transpose(0, 1, 3, 2, 4).reshape(3, 2, N_DOM, SLOTS)
    sources = jnp.broadcast_to(intersection_source.reshape(1, 2, N_DOM, INTERSECTIONS * ROWS), (3, 2, N_DOM, INTERSECTIONS * ROWS))
    values = jnp.take_along_axis(incoming, sources, axis=3).reshape(3, 2, N_DOM, ROWS, INTERSECTIONS)
    weights = intersection_weight.reshape(2, N_DOM, ROWS, INTERSECTIONS)
    regrid = lax.optimization_barrier(jnp.sum(values * weights, axis=-1)) / lax.optimization_barrier(jnp.sum(weights, axis=-1))
    atmosphere = blocks[:, :, 0].reshape(3, LEV, N_DOM * XP, YP)
    metric = atm_metric.reshape(2, N_DOM * XP, YP)
    stepped = dycore(atmosphere, metric[0], metric[1], wave_speed)
    averaged = average_second(average_first(stepped, jnp.roll(stepped, 1, axis=2), jnp.roll(stepped, -1, axis=2)))
    atmosphere_new = averaged.reshape(3, LEV, N_DOM, ROWS)
    ocean = blocks[:, :, 1]
    edges = ocean_edges.reshape(2, N_DOM, YP)
    left_values = jnp.take_along_axis(ocean, jnp.broadcast_to(edges[0], (3, LEV, N_DOM, YP)), axis=3)
    right_values = jnp.take_along_axis(ocean, jnp.broadcast_to(edges[1], (3, LEV, N_DOM, YP)), axis=3)
    extended = jnp.concatenate([ocean, jnp.roll(right_values, 1, axis=2), jnp.roll(left_values, -1, axis=2)], axis=3)
    adjacency = ocean_adjacent.reshape(6, N_DOM, ROWS)
    summed = jnp.zeros(ocean.shape, jnp.float32)
    for neighbor in range(6):
        gathered = jnp.take_along_axis(extended, jnp.broadcast_to(adjacency[neighbor], (3, LEV, N_DOM, ROWS)), axis=3)
        summed = summed + (gathered - ocean)
    ocean_new = ocean + ocean_kappa.reshape(N_DOM, ROWS) * summed
    updated = jnp.stack([atmosphere_new, ocean_new], axis=2)
    rates = couple_rate.T[:, :, None, None]
    surface_top = updated[:, LEV - 1]
    surface_top = surface_top + rates * (regrid - surface_top)
    updated = updated.at[:, LEV - 1].set(surface_top)
    return updated.reshape(3, LEV, 2 * N_DOM * ROWS)
```

```python
import functools
import jax
import jax.numpy as jnp
import numpy as np
from jax import lax
from jax.experimental import pallas as pl
from jax.experimental.pallas import tpu as pltpu
from jax.sharding import PartitionSpec as P

TIME_STEP = 0.05
LANES = 128
VMEM = pl.BlockSpec(memory_space=pltpu.VMEM)
SMEM = pl.BlockSpec(memory_space=pltpu.SMEM)
HBM = pl.BlockSpec(memory_space=pltpu.HBM)
PARAMS = dict(vmem_limit_bytes=24 << 20)


def gll_derivative():
    nodes = np.array([-1.0, -1.0 / np.sqrt(5.0), 1.0 / np.sqrt(5.0), 1.0])
    barycentric = np.array(
        [1.0 / np.prod([nodes[i] - nodes[j] for j in range(4) if j != i]) for i in range(4)]
    )
    matrix = np.zeros((4, 4))
    for i in range(4):
        for j in range(4):
            if i != j:
                matrix[i, j] = barycentric[j] / barycentric[i] / (nodes[i] - nodes[j])
        matrix[i, i] = -np.sum(matrix[i])
    return matrix


DERIVATIVE = gll_derivative()


def lane_phase(shape):
    return lax.broadcasted_iota(jnp.int32, shape, 1) % 4


def along_second(value, phase):
    width = value.shape[1]
    total = jnp.zeros_like(value)
    for shift in range(-3, 4):
        factor = jnp.zeros(value.shape, jnp.float32)
        for i in range(4):
            if 0 <= i + shift < 4:
                factor = jnp.where(phase == i, np.float32(DERIVATIVE[i, i + shift]), factor)
        moved = value if shift == 0 else pltpu.roll(value, (-shift) % width, 1)
        total = total + factor * moved
    return total


def advance(x_points, y_points, state_ref, metric_ref, speed_ref, stepped_ref):
    level = lax.broadcasted_iota(jnp.int32, (state_ref.shape[1], LANES), 0)
    speed = jnp.zeros(level.shape, jnp.float32)
    for k in range(level.shape[0]):
        speed = jnp.where(level == k, speed_ref[k], speed)

    def piece(g, _):
        def at(i, f):
            return state_ref[f, :, pl.ds(pl.multiple_of(start + i * y_points, LANES), LANES)]

        start = (g // (y_points // LANES)) * 4 * y_points + (g % (y_points // LANES)) * LANES
        phase = lane_phase((state_ref.shape[1], LANES))
        u = [at(i, 0) for i in range(4)]
        v = [at(i, 1) for i in range(4)]
        h = [at(i, 2) for i in range(4)]
        for i in range(4):
            here = pl.ds(pl.multiple_of(start + i * y_points, LANES), LANES)
            gx = metric_ref[0:1, here]
            gy = metric_ref[1:2, here]
            dx_h = sum(np.float32(DERIVATIVE[i, j]) * h[j] for j in range(4))
            dx_u = sum(np.float32(DERIVATIVE[i, j]) * u[j] for j in range(4))
            stepped_ref[0, :, here] = u[i] - TIME_STEP * (gx * dx_h)
            stepped_ref[1, :, here] = v[i] - TIME_STEP * (gy * along_second(h[i], phase))
            spread = gx * dx_u + gy * along_second(v[i], phase)
            stepped_ref[2, :, here] = h[i] - TIME_STEP * speed * spread
        return 0

    lax.fori_loop(0, x_points // 4 * (y_points // LANES), piece, 0)


CHUNK = 32
KEEP = 32


def two_terms(table):
    high = table.astype(jnp.bfloat16)
    low = (table - high.astype(jnp.float32)).astype(jnp.bfloat16)
    return jnp.concatenate([high, low], axis=1)


def pick(terms, depth, low, high):
    count = low.shape[1]
    low = jnp.broadcast_to(low.astype(jnp.int16), (LANES, count))
    lane = lax.broadcasted_iota(jnp.int16, (LANES, LANES), 0)
    lane = jnp.concatenate([lane] * (count // LANES), axis=1)
    hot = jnp.where(lane == low, jnp.bfloat16(1), jnp.bfloat16(0))
    found = jnp.dot(terms, jnp.concatenate([hot, hot], axis=0), preferred_element_type=jnp.float32)
    high = jnp.broadcast_to(high, (8, count))
    own = lax.broadcasted_iota(jnp.int32, high.shape, 0) == (high & 7)
    picked = []
    for f in range(3):
        parts = [found[f * depth + 8 * i : f * depth + 8 * i + 8] for i in range(depth // 8)]
        bit = 3
        while len(parts) > 1:
            odd = ((high >> bit) & 1) == 1
            parts = [jnp.where(odd, parts[i + 1], parts[i]) for i in range(0, len(parts), 2)]
            bit += 1
        picked.append(jnp.sum(jnp.where(own, parts[0], 0.0), axis=0, keepdims=True))
    return picked


def row_of(ref, start, count):
    return jnp.concatenate([ref[pl.ds(start + r, 1), :] for r in range(count)], axis=1)


def split_pairs(source_ref, weight_ref, low_ref, high_ref, share_ref):
    i = lax.broadcasted_iota(jnp.int32, (LANES, LANES), 0)
    j = lax.broadcasted_iota(jnp.int32, (LANES, LANES), 1)
    half = LANES // 2
    chosen = (i == 2 * (j % half) + j // half).astype(jnp.float32).astype(jnp.bfloat16)

    def move(value):
        return jnp.dot(value.astype(jnp.bfloat16), chosen, preferred_element_type=jnp.float32)

    source = source_ref[...]
    low_ref[...] = (move((source & (LANES - 1)).astype(jnp.float32)) + 0.5).astype(jnp.int32)
    high_ref[...] = (move((source >> 7).astype(jnp.float32)) + 0.5).astype(jnp.int32)
    weight = weight_ref[...]
    upper = weight.astype(jnp.bfloat16).astype(jnp.float32)
    share_ref[...] = move(upper) + move(weight - upper)


def regrid_into(regrid_ref, arrived, low_ref, high_ref, share_ref, terms_ref, value_ref):
    depth = low_ref.shape[0]
    for f in range(3):
        terms_ref[f * depth : (f + 1) * depth, :] = two_terms(arrived(f).reshape(depth, LANES))

    def step(c, _):
        low, high = row_of(low_ref, c * CHUNK, CHUNK), row_of(high_ref, c * CHUNK, CHUNK)
        values = pick(terms_ref[...], depth, low, high)
        for f in range(3):
            for r in range(CHUNK):
                value_ref[f, pl.ds(c * CHUNK + r, 1), :] = values[f][:, r * LANES : (r + 1) * LANES]
        return 0

    lax.fori_loop(0, depth // CHUNK, step, 0)
    share = share_ref[...]
    whole = share + pltpu.roll(share, LANES // 2, 1)
    first = lax.broadcasted_iota(jnp.int32, (depth // 2, LANES), 1) < LANES // 2
    for f in range(3):
        product = value_ref[f] * share
        share_ref[...] = (product + pltpu.roll(product, LANES // 2, 1)) / whole
        even = share_ref[pl.ds(0, depth // 2, stride=2), :]
        odd = share_ref[pl.ds(1, depth // 2, stride=2), :]
        regrid_ref[f] = jnp.where(first, even, odd)


def to_rows(source_ref, source_at, table_ref, table_at, count, name_at, unroll):
    def piece(c, _):
        here = pl.ds(pl.multiple_of(source_at + c * LANES, LANES), LANES)
        name = lax.broadcasted_iota(jnp.int32, (8, LANES), 1) + (name_at + c * LANES)
        kind = lax.broadcasted_iota(jnp.int32, (8, LANES), 0)
        name = jnp.where(kind < 6, name, jnp.where(kind == 6, 1, 0)).astype(jnp.float32)
        block = jnp.concatenate([source_ref[f, :, here] for f in range(3)] + [name], axis=0)
        there = pl.ds(pl.multiple_of(table_at + c * LANES, 8), LANES)
        table_ref[there, :KEEP] = jnp.transpose(block)
        return 0

    lax.fori_loop(0, count // LANES, piece, 0, unroll=unroll)


def walk(y_points, x_points, next_ref, edges_ref, visit, middle):
    def chain(c, _):
        base = pl.multiple_of(c * 16, 16)
        places = [edges_ref[0, base + u] for u in range(16)]
        for x in range(x_points - 1):
            if x or not middle:
                for u in range(16):
                    visit(x, base, u, places[u])
            if x < x_points - 2:
                places = [next_ref[place] for place in places]
        if not middle:
            for u in range(16):
                visit(x_points - 1, base, u, edges_ref[1, base + u])
        return 0

    lax.fori_loop(0, y_points // 16, chain, 0)


def start_kernel(
    n, x_points, y_points, state_hbm, rows_hbm, source_hbm, weight_hbm, metric_hbm, adjacent_hbm, edges_hbm, speed_hbm,
    state_ref, in_ref, regrid_ref, stepped_ref, west_ref, east_ref, table_ref, grid_ref,
    rows_ref, metric_ref, source_ref, weight_ref, low_ref, high_ref, share_ref, value_ref, made_ref,
    surface_ref, terms_ref, pair_terms_ref, out_ref, rim_ref, next_ref, edges_ref, speed_ref,
    load_sem, slot_send, slot_recv, edge_send, edge_recv, pair_send, pair_recv, made_send, made_recv,
):
    sec, dom = lax.axis_index("sec"), lax.axis_index("dom")
    right, left = lax.rem(dom + 1, n), lax.rem(dom + n - 1, n)
    mesh_ids = pl.DeviceIdType.MESH
    atmosphere, ocean = sec == 0, sec == 1
    load_state = pltpu.make_async_copy(state_hbm, state_ref, load_sem.at[0])
    load_rows = pltpu.make_async_copy(rows_hbm, rows_ref, load_sem.at[1])
    load_metric = pltpu.make_async_copy(metric_hbm, metric_ref, load_sem.at[2])
    load_next = pltpu.make_async_copy(adjacent_hbm.at[2], next_ref, load_sem.at[3])
    load_edges = pltpu.make_async_copy(edges_hbm, edges_ref, load_sem.at[4])
    load_speed = pltpu.make_async_copy(speed_hbm, speed_ref, load_sem.at[5])
    load_state.start()
    load_rows.start()
    barrier = pltpu.get_barrier_semaphore()

    def hello(a, b):
        pl.semaphore_signal(barrier, inc=1, device_id=(a, b), device_id_type=mesh_ids)

    @pl.when(atmosphere)
    def _():
        load_metric.start()
        load_speed.start()

        def greet(p, _):
            hello(1, p)

            @pl.when(p != dom)
            def _():
                hello(0, p)

            return 0

        lax.fori_loop(0, n, greet, 0)

    @pl.when(ocean)
    def _():
        load_edges.start()
        load_next.start()
        hello(0, dom)
        hello(1, left)
        hello(1, right)

    load_state.wait()
    depth, top = state_ref.shape[2] // LANES, state_ref.shape[1] - 1
    for f in range(3):
        for h in range(depth):
            surface_ref[f * depth + h : f * depth + h + 1, :] = state_ref[
                f, top : top + 1, h * LANES : (h + 1) * LANES
            ]
    terms_ref[...] = two_terms(surface_ref[...])
    load_rows.wait()

    def remote(source, target, send, recv, device):
        return pltpu.make_async_remote_copy(
            src_ref=source, dst_ref=target, send_sem=send, recv_sem=recv, device_id=device, device_id_type=mesh_ids
        )

    pair_source = remote(source_hbm, source_ref, pair_send.at[0], pair_recv.at[0], (0, dom))
    pair_weight = remote(weight_hbm, weight_ref, pair_send.at[1], pair_recv.at[1], (0, dom))

    @pl.when(atmosphere)
    def _():
        pl.semaphore_wait(barrier, n)

    @pl.when(ocean)
    def _():
        pl.semaphore_wait(barrier, n + 2)
        pair_source.start()
        pair_weight.start()

    lines = out_ref.shape[2]
    peers = CHUNK // lines

    def slots(p):
        return remote(out_ref.at[p], in_ref.at[sec, dom], slot_send.at[p], slot_recv.at[sec, dom], (0, p))

    def own_slots():
        return pltpu.make_async_copy(out_ref.at[dom], in_ref.at[0, dom], slot_recv.at[0, dom])

    chunks = rows_ref.shape[0] // CHUNK

    def send(k, _):
        c = lax.rem(k + dom * chunks // n, chunks)
        index = row_of(rows_ref, c * CHUNK, CHUNK)
        values = pick(terms_ref[...], depth, index & (LANES - 1), index >> 7)
        for f in range(3):
            for r in range(CHUNK):
                out_ref[c * peers + r // lines, f, pl.ds(r % lines, 1), :] = values[f][:, r * LANES : (r + 1) * LANES]

        def ship(j, _):
            p = c * peers + j
            here = jnp.logical_and(atmosphere, p == dom)

            @pl.when(here)
            def _():
                own_slots().start()

            @pl.when(jnp.logical_not(here))
            def _():
                slots(p).start()

            return 0

        lax.fori_loop(0, peers, ship, 0)
        return 0

    lax.fori_loop(0, chunks, send, 0)

    rows = state_ref.shape[2]
    first, last = pl.ds(0, y_points), pl.ds(rows - y_points, y_points)
    rim_first, rim_last = rim_ref.at[:, :, first], rim_ref.at[:, :, pl.ds(y_points, y_points)]
    air_edges = [
        remote(stepped_ref.at[:, :, last], west_ref, edge_send.at[0], edge_recv.at[0], (0, right)),
        remote(stepped_ref.at[:, :, first], east_ref, edge_send.at[1], edge_recv.at[1], (0, left)),
    ]
    sea_edges = [
        remote(rim_last, west_ref, edge_send.at[0], edge_recv.at[0], (1, right)),
        remote(rim_first, east_ref, edge_send.at[1], edge_recv.at[1], (1, left)),
    ]
    made = remote(made_ref, regrid_ref, made_send, made_recv, (1, dom))

    def sent(p, _):
        @pl.when(jnp.logical_not(jnp.logical_and(atmosphere, p == dom)))
        def _():
            slots(p).wait_send()

        return 0

    def arrived_from(a):
        def wait(p, _):
            def arrival():
                remote(out_ref.at[p], in_ref.at[a, p], slot_send.at[p], slot_recv.at[a, p], (0, p)).wait_recv()

            if a:
                arrival()
            else:

                @pl.when(p == dom)
                def _():
                    own_slots().wait()

                @pl.when(p != dom)
                def _():
                    arrival()

            return 0

        lax.fori_loop(0, n, wait, 0)

    @pl.when(atmosphere)
    def _():
        load_metric.wait()
        load_speed.wait()
        advance(x_points, y_points, state_ref, metric_ref, speed_ref, stepped_ref)
        for each in air_edges:
            each.start()
        pair_source.wait_recv()
        pair_weight.wait_recv()
        split_pairs(source_ref, weight_ref, low_ref, high_ref, share_ref)
        arrived_from(0)
        regrid_into(made_ref, lambda f: in_ref[0, :, f], low_ref, high_ref, share_ref, pair_terms_ref, value_ref)
        made.start()
        arrived_from(1)
        for each in air_edges:
            each.wait()
        lax.fori_loop(0, n, sent, 0)
        made.wait_send()

    @pl.when(ocean)
    def _():
        to_rows(state_ref, 0, table_ref, 0, rows, 0, 8)
        load_edges.wait()

        def column(x, u):
            return pl.ds(8 + (x + 1) * y_points + u, 1)

        def edge(c, _):
            base = pl.multiple_of(c * 16, 16)
            for k, x in ((0, 0), (1, x_points - 1)):
                places = [edges_ref[k, base + u] for u in range(16)]
                for u in range(16):
                    grid_ref[column(x, base + u), :] = table_ref[pl.ds(places[u], 1), :]
            return 0

        lax.fori_loop(0, y_points // 16, edge, 0)
        for k, x in ((0, 0), (1, x_points - 1)):
            for c in range(y_points // LANES):
                at = 8 + (x + 1) * y_points + c * LANES
                block = jnp.transpose(grid_ref[at : at + LANES, :KEEP])
                for f in range(3):
                    levels = top + 1
                    rim_ref[f, :, k * y_points + c * LANES : k * y_points + (c + 1) * LANES] = block[
                        f * levels : (f + 1) * levels
                    ]
        for each in sea_edges:
            each.start()
        load_next.wait()

        def visit(x, base, u, place):
            grid_ref[column(x, base + u), :] = table_ref[pl.ds(place, 1), :]

        walk(y_points, x_points, next_ref, edges_ref, visit, True)
        pair_source.wait_send()
        pair_weight.wait_send()
        for each in sea_edges:
            each.wait()
        lax.fori_loop(0, n, sent, 0)
        made.wait_recv()


def sum_neighbours(x_points, y_points, grid_ref, rims, sum_ref):
    lane = lax.broadcasted_iota(jnp.int32, (8, LANES), 1)
    row = lax.broadcasted_iota(jnp.int32, (8, LANES), 0)

    def mask(*names):
        kept = lane < 24
        for name in names:
            kept = kept | (lane == 24 + name)
        return kept.astype(jnp.float32)

    same, tilted = mask(2, 3), mask(4, 5)
    above, below = mask(0), mask(1)
    east, west = mask(2, 4), mask(3, 5)

    def read(x, at, shift):
        if 0 <= x < x_points:
            return grid_ref[pl.ds(8 + (x + 1) * y_points + at + shift, 8), :]
        return rims[0 if x < 0 else 1][pl.ds(8 + at + shift, 8), :]

    def inner(c, _):
        at = c * 8
        joined = {}
        for x in range(-1, x_points + 1):
            tilt = -1 if x % 2 else 1
            joined[x] = read(x, at, 0) * same + read(x, at, tilt) * tilted
            if x > 0:
                upright = read(x - 1, at, 1) * above + read(x - 1, at, -1) * below
                total = upright + joined[x] * east + joined[x - 2] * west
                sum_ref[pl.ds(pl.multiple_of((x - 1) * y_points + at, 8), 8), :] = total
        return 0

    lax.fori_loop(1, y_points // 8 - 1, inner, 0)

    for at, gone, missing in ((0, row == 0, -1), (y_points - 8, row == 7, 1)):
        for x in range(x_points):
            own = read(x, at, 0)
            tilt = 1 if x % 2 else -1

            def near(x, shift):
                value = read(x, at, shift)
                return jnp.where(gone, own, value) if shift == missing else value

            total = near(x, 1) * above + near(x, -1) * below
            total = total + (near(x + 1, 0) * same + near(x + 1, tilt) * tilted) * east
            total = total + (near(x - 1, 0) * same + near(x - 1, tilt) * tilted) * west
            sum_ref[x * y_points + at : x * y_points + at + 8, :] = total


def end_kernel(
    x_points, y_points, state_ref, in_ref, regrid_in_ref, stepped_ref, west_ref, east_ref, table_in_ref, grid_ref,
    source_hbm, weight_hbm, kappa_hbm, adjacent_hbm, edges_hbm, rate_hbm,
    new_hbm, table_ref,
    new_ref, source_ref, weight_ref, low_ref, high_ref, share_ref, value_ref, pair_terms_ref, regrid_ref,
    kappa_ref, adjacent_ref, next_ref, few_ref, west_rim_ref, east_rim_ref, sum_ref, edges_ref, rate_ref,
    load_sem, store_sem,
):
    sec = lax.axis_index("sec")
    load_rate = pltpu.make_async_copy(rate_hbm, rate_ref, load_sem.at[5])
    load_rate.start()
    levels, rows = state_ref.shape[1], state_ref.shape[2]

    def couple(f, here, value, relaxed):
        row = lax.broadcasted_iota(jnp.int32, value.shape, 0)
        new_ref[f, :, here] = jnp.where(row == levels - 1, value + rate_ref[0, f] * (relaxed - value), value)

    @pl.when(sec == 0)
    def _():
        load_source = pltpu.make_async_copy(source_hbm, source_ref, load_sem.at[0])
        load_weight = pltpu.make_async_copy(weight_hbm, weight_ref, load_sem.at[1])
        load_source.start()
        load_weight.start()
        load_source.wait()
        load_weight.wait()
        load_rate.wait()
        split_pairs(source_ref, weight_ref, low_ref, high_ref, share_ref)
        regrid_into(regrid_ref, lambda f: in_ref[1, :, f], low_ref, high_ref, share_ref, pair_terms_ref, value_ref)
        stores = [pltpu.make_async_copy(new_ref.at[f], new_hbm.at[f], store_sem.at[f]) for f in range(3)]
        for f in range(3):
            for x in range(x_points):
                here = slice(x * y_points, (x + 1) * y_points)
                value = stepped_ref[f, :, here]
                if x % 4 == 3:
                    other = (
                        stepped_ref[f, :, (x + 1) * y_points : (x + 2) * y_points]
                        if x < x_points - 1
                        else east_ref[f]
                    )
                    value = (value + other) * 0.5
                elif x % 4 == 0:
                    other = stepped_ref[f, :, (x - 1) * y_points : x * y_points] if x else west_ref[f]
                    value = (value + other) * 0.5
                position = lax.broadcasted_iota(jnp.int32, value.shape, 1)
                phase = position % 4
                after = pltpu.roll(value, y_points - 1, 1)
                before = pltpu.roll(value, 1, 1)
                averaged = jnp.where(
                    (phase == 3) & (position < y_points - 1),
                    (value + after) * 0.5,
                    jnp.where((phase == 0) & (position > 0), (value + before) * 0.5, value),
                )
                lines = y_points // LANES
                relaxed = jnp.concatenate(
                    [regrid_ref[f, x * lines + i : x * lines + i + 1, :] for i in range(lines)], axis=1
                )
                couple(f, here, averaged, relaxed)
            stores[f].start()
        for each in stores:
            each.wait()

    @pl.when(sec == 1)
    def _():
        load_next = pltpu.make_async_copy(adjacent_hbm.at[2], next_ref, load_sem.at[0])
        load_adjacent = pltpu.make_async_copy(adjacent_hbm, adjacent_ref, load_sem.at[1])
        load_kappa = pltpu.make_async_copy(kappa_hbm, kappa_ref, load_sem.at[2])
        load_edges = pltpu.make_async_copy(edges_hbm, edges_ref, load_sem.at[4])
        load_edges.start()
        load_next.start()
        load_adjacent.start()
        load_kappa.start()
        to_rows(west_ref, 0, west_rim_ref, 8, y_points, rows, 4)
        to_rows(east_ref, 0, east_rim_ref, 8, y_points, rows + y_points, 4)
        sum_neighbours(x_points, y_points, grid_ref, (west_rim_ref, east_rim_ref), sum_ref)
        load_next.wait()
        load_edges.wait()
        load_rate.wait()

        def visit(x, base, u, place):
            table_ref[pl.ds(place, 1), :] = sum_ref[pl.ds(x * y_points + base + u, 1), :]

        walk(y_points, x_points, next_ref, edges_ref, visit, False)
        load_adjacent.wait()
        load_kappa.wait()
        part = rows // 4
        stores = [
            pltpu.make_async_copy(
                new_ref.at[:, :, pl.ds(k * part, part)], new_hbm.at[:, :, pl.ds(k * part, part)], store_sem.at[k]
            )
            for k in range(4)
        ]

        def finish(c, wrong):
            here = pl.ds(pl.multiple_of(c * LANES, LANES), LANES)
            block = jnp.transpose(table_ref[here, :KEEP])
            kappa = kappa_ref[pl.ds(c, 1), :]
            for f in range(3):
                value = state_ref[f, :, here]
                swept = value + kappa * (block[f * levels : (f + 1) * levels] - 6.0 * value)
                couple(f, here, swept, regrid_in_ref[f, pl.ds(c, 1), :])
            named = adjacent_ref[:, here].astype(jnp.float32)
            names = block[24:32]
            off = (names[0:6] != named).astype(jnp.float32)
            return jnp.maximum(wrong, jnp.maximum(jnp.max(off, axis=0, keepdims=True), names[6:7]))

        wrong = jnp.zeros((1, LANES), jnp.float32)
        for k in range(4):
            blocks = part // LANES
            wrong = lax.fori_loop(k * blocks, (k + 1) * blocks, finish, wrong, unroll=8)
            stores[k].start()
        for each in stores:
            each.wait()

        @pl.when(jnp.max(wrong) > 0.0)
        def _():
            to_rows(state_ref, 0, sum_ref, 0, rows, 0, 1)
            to_rows(west_ref, 0, sum_ref, rows, y_points, rows, 1)
            to_rows(east_ref, 0, sum_ref, rows + y_points, y_points, rows + y_points, 1)

            def block(c, _):
                fetch = pltpu.make_async_copy(
                    adjacent_hbm.at[:, pl.ds(pl.multiple_of(c * LANES, LANES), LANES)], few_ref, load_sem.at[3]
                )
                fetch.start()
                fetch.wait()

                def cell(i, _):
                    total = sum_ref[pl.ds(few_ref[0, i], 1), :]
                    for j in range(1, 6):
                        total = total + sum_ref[pl.ds(few_ref[j, i], 1), :]
                    table_ref[pl.ds(c * LANES + i, 1), :] = total
                    return 0

                lax.fori_loop(0, LANES, cell, 0)
                return 0

            lax.fori_loop(0, rows // LANES, block, 0)
            lax.fori_loop(0, rows // LANES, finish, wrong)
            whole = pltpu.make_async_copy(new_ref, new_hbm, store_sem.at[0])
            whole.start()
            whole.wait()


def body(
    state, send_rows, intersection_source, intersection_weight, couple_rate, atm_metric, wave_speed,
    ocean_adjacent, ocean_edges, ocean_kappa,
):
    levels, rows = state.shape[1], state.shape[2]
    y_points = ocean_edges.shape[1]
    x_points = rows // y_points
    n = lax.axis_size("dom")
    slots = send_rows.shape[0]
    lines = slots // n // LANES
    f32, i32 = jnp.float32, jnp.int32
    pairs = slots // LANES
    source, weight = intersection_source.reshape(-1, LANES), intersection_weight.reshape(-1, LANES)
    placed, slot_rows, source, weight, metric, adjacent, kappa, edges, speed, rate = [
        pltpu.with_memory_space_constraint(each, pltpu.HBM)
        for each in (
            state, send_rows.reshape(-1, LANES), source, weight, atm_metric, ocean_adjacent,
            ocean_kappa.reshape(-1, LANES), ocean_edges, wave_speed, couple_rate,
        )
    ]

    border = jax.ShapeDtypeStruct((3, levels, y_points), f32)
    whole = jax.ShapeDtypeStruct(state.shape, f32)
    table = jax.ShapeDtypeStruct((rows, LANES), f32)
    made = jax.ShapeDtypeStruct((3, rows // LANES, LANES), f32)
    pair_scratch = [
        pltpu.VMEM((pairs, LANES), i32),
        pltpu.VMEM((pairs, LANES), f32),
        pltpu.VMEM((pairs, LANES), i32),
        pltpu.VMEM((pairs, LANES), i32),
        pltpu.VMEM((pairs, LANES), f32),
        pltpu.VMEM((3, pairs, LANES), f32),
    ]
    dma = pltpu.SemaphoreType.DMA
    held, incoming, regrid, stepped, west, east, cells, grid = pl.pallas_call(
        functools.partial(start_kernel, n, x_points, y_points),
        out_shape=[
            whole,
            jax.ShapeDtypeStruct((2, n, 3, lines, LANES), f32),
            made,
            whole,
            border,
            border,
            table,
            jax.ShapeDtypeStruct(((x_points + 2) * y_points + 16, LANES), f32),
        ],
        in_specs=[HBM] * 8,
        out_specs=[VMEM] * 8,
        scratch_shapes=[
            pltpu.VMEM((pairs, LANES), i32),
            pltpu.VMEM(atm_metric.shape, f32),
            *pair_scratch,
            pltpu.VMEM(made.shape, f32),
            pltpu.VMEM((3 * rows // LANES, LANES), f32),
            pltpu.VMEM((3 * rows // LANES, 2 * LANES), jnp.bfloat16),
            pltpu.VMEM((3 * pairs, 2 * LANES), jnp.bfloat16),
            pltpu.VMEM((n, 3, lines, LANES), f32),
            pltpu.VMEM((3, levels, 2 * y_points), f32),
            pltpu.SMEM((rows,), i32),
            pltpu.SMEM(ocean_edges.shape, i32),
            pltpu.SMEM(wave_speed.shape, f32),
            dma((6,)),
            dma((n,)),
            dma((2, n)),
            dma((2,)),
            dma((2,)),
            dma((2,)),
            dma((2,)),
            dma,
            dma,
        ],
        compiler_params=pltpu.CompilerParams(collective_id=0, has_side_effects=True, **PARAMS),
        name="start",
    )(
        placed, slot_rows, source, weight, metric, adjacent, edges, speed,
    )

    new_state, _ = pl.pallas_call(
        functools.partial(end_kernel, x_points, y_points),
        out_shape=[whole, table],
        in_specs=[VMEM] * 8 + [HBM] * 6,
        out_specs=[HBM, VMEM],
        input_output_aliases={6: 1},
        scratch_shapes=[
            pltpu.VMEM(state.shape, f32),
            *pair_scratch,
            pltpu.VMEM((3 * pairs, 2 * LANES), jnp.bfloat16),
            pltpu.VMEM(made.shape, f32),
            pltpu.VMEM((rows // LANES, LANES), f32),
            pltpu.VMEM(ocean_adjacent.shape, i32),
            pltpu.SMEM((rows,), i32),
            pltpu.SMEM((6, LANES), i32),
            pltpu.VMEM((y_points + 16, LANES), f32),
            pltpu.VMEM((y_points + 16, LANES), f32),
            pltpu.VMEM((rows + 2 * y_points, LANES), f32),
            pltpu.SMEM(ocean_edges.shape, i32),
            pltpu.SMEM(couple_rate.shape, f32),
            dma((6,)),
            dma((4,)),
        ],
        compiler_params=pltpu.CompilerParams(**PARAMS),
        name="end",
    )(
        held, incoming, regrid, stepped, west, east, cells, grid,
        source, weight, kappa, adjacent, edges, rate,
    )
    return new_state


def solution(mesh):
    in_specs = (
        P(None, None, ("sec", "dom")),
        P(("sec", "dom")),
        P(("sec", "dom")),
        P(("sec", "dom")),
        P("sec", None),
        P(None, "dom"),
        P(),
        P(None, "dom"),
        P(None, "dom"),
        P("dom"),
    )
    out_specs = P(None, None, ("sec", "dom"))
    return jax.shard_map(body, mesh=mesh, in_specs=in_specs, out_specs=out_specs, check_vma=False)
```

```python
import functools
import jax
import jax.numpy as jnp
import numpy as np
from jax import lax
from jax.experimental import pallas as pl
from jax.experimental.pallas import tpu as pltpu
from jax.sharding import PartitionSpec as P

TIME_STEP = 0.05
LANES = 128
VMEM = pl.BlockSpec(memory_space=pltpu.VMEM)
SMEM = pl.BlockSpec(memory_space=pltpu.SMEM)
HBM = pl.BlockSpec(memory_space=pltpu.HBM)
PARAMS = dict(vmem_limit_bytes=24 << 20)


def gll_derivative():
    nodes = np.array([-1.0, -1.0 / np.sqrt(5.0), 1.0 / np.sqrt(5.0), 1.0])
    barycentric = np.array(
        [1.0 / np.prod([nodes[i] - nodes[j] for j in range(4) if j != i]) for i in range(4)]
    )
    matrix = np.zeros((4, 4))
    for i in range(4):
        for j in range(4):
            if i != j:
                matrix[i, j] = barycentric[j] / barycentric[i] / (nodes[i] - nodes[j])
        matrix[i, i] = -np.sum(matrix[i])
    return matrix


DERIVATIVE = gll_derivative()


def lane_phase(shape):
    return lax.broadcasted_iota(jnp.int32, shape, 1) % 4


def along_second(value, phase):
    width = value.shape[1]
    total = jnp.zeros_like(value)
    for shift in range(-3, 4):
        factor = jnp.zeros(value.shape, jnp.float32)
        for i in range(4):
            if 0 <= i + shift < 4:
                factor = jnp.where(phase == i, np.float32(DERIVATIVE[i, i + shift]), factor)
        moved = value if shift == 0 else pltpu.roll(value, (-shift) % width, 1)
        total = total + factor * moved
    return total


def advance(x_points, y_points, state_ref, metric_ref, speed_ref, stepped_ref):
    level = lax.broadcasted_iota(jnp.int32, (state_ref.shape[1], LANES), 0)
    speed = jnp.zeros(level.shape, jnp.float32)
    for k in range(level.shape[0]):
        speed = jnp.where(level == k, speed_ref[k], speed)

    def piece(g, _):
        def at(i, f):
            return state_ref[f, :, pl.ds(pl.multiple_of(start + i * y_points, LANES), LANES)]

        start = (g // (y_points // LANES)) * 4 * y_points + (g % (y_points // LANES)) * LANES
        phase = lane_phase((state_ref.shape[1], LANES))
        u = [at(i, 0) for i in range(4)]
        v = [at(i, 1) for i in range(4)]
        h = [at(i, 2) for i in range(4)]
        for i in range(4):
            here = pl.ds(pl.multiple_of(start + i * y_points, LANES), LANES)
            gx = metric_ref[0:1, here]
            gy = metric_ref[1:2, here]
            dx_h = sum(np.float32(DERIVATIVE[i, j]) * h[j] for j in range(4))
            dx_u = sum(np.float32(DERIVATIVE[i, j]) * u[j] for j in range(4))
            stepped_ref[0, :, here] = u[i] - TIME_STEP * (gx * dx_h)
            stepped_ref[1, :, here] = v[i] - TIME_STEP * (gy * along_second(h[i], phase))
            spread = gx * dx_u + gy * along_second(v[i], phase)
            stepped_ref[2, :, here] = h[i] - TIME_STEP * speed * spread
        return 0

    lax.fori_loop(0, x_points // 4 * (y_points // LANES), piece, 0)


CHUNK = 32
KEEP = 32


def two_terms(table):
    high = table.astype(jnp.bfloat16)
    low = (table - high.astype(jnp.float32)).astype(jnp.bfloat16)
    return jnp.concatenate([high, low], axis=1)


def pick(terms, depth, low, high):
    count = low.shape[1]
    low = jnp.broadcast_to(low.astype(jnp.int16), (LANES, count))
    lane = lax.broadcasted_iota(jnp.int16, (LANES, LANES), 0)
    lane = jnp.concatenate([lane] * (count // LANES), axis=1)
    hot = jnp.where(lane == low, jnp.bfloat16(1), jnp.bfloat16(0))
    found = jnp.dot(terms, jnp.concatenate([hot, hot], axis=0), preferred_element_type=jnp.float32)
    high = jnp.broadcast_to(high, (8, count))
    own = lax.broadcasted_iota(jnp.int32, high.shape, 0) == (high & 7)
    picked = []
    for f in range(3):
        parts = [found[f * depth + 8 * i : f * depth + 8 * i + 8] for i in range(depth // 8)]
        bit = 3
        while len(parts) > 1:
            odd = ((high >> bit) & 1) == 1
            parts = [jnp.where(odd, parts[i + 1], parts[i]) for i in range(0, len(parts), 2)]
            bit += 1
        picked.append(jnp.sum(jnp.where(own, parts[0], 0.0), axis=0, keepdims=True))
    return picked


def row_of(ref, start, count):
    return jnp.concatenate([ref[pl.ds(start + r, 1), :] for r in range(count)], axis=1)


def split_pairs(source_ref, weight_ref, low_ref, high_ref, share_ref):
    i = lax.broadcasted_iota(jnp.int32, (LANES, LANES), 0)
    j = lax.broadcasted_iota(jnp.int32, (LANES, LANES), 1)
    half = LANES // 2
    chosen = (i == 2 * (j % half) + j // half).astype(jnp.float32).astype(jnp.bfloat16)

    def move(value):
        return jnp.dot(value.astype(jnp.bfloat16), chosen, preferred_element_type=jnp.float32)

    source = source_ref[...]
    low_ref[...] = (move((source & (LANES - 1)).astype(jnp.float32)) + 0.5).astype(jnp.int32)
    high_ref[...] = (move((source >> 7).astype(jnp.float32)) + 0.5).astype(jnp.int32)
    weight = weight_ref[...]
    upper = weight.astype(jnp.bfloat16).astype(jnp.float32)
    share_ref[...] = move(upper) + move(weight - upper)


def regrid_into(regrid_ref, arrived, low_ref, high_ref, share_ref, terms_ref, value_ref, ratio_ref):
    depth = low_ref.shape[0]
    for f in range(3):
        terms_ref[f * depth : (f + 1) * depth, :] = two_terms(arrived(f).reshape(depth, LANES))

    def step(c, _):
        low, high = row_of(low_ref, c * CHUNK, CHUNK), row_of(high_ref, c * CHUNK, CHUNK)
        values = pick(terms_ref[...], depth, low, high)
        for f in range(3):
            for r in range(CHUNK):
                value_ref[f, pl.ds(c * CHUNK + r, 1), :] = values[f][:, r * LANES : (r + 1) * LANES]
        return 0

    lax.fori_loop(0, depth // CHUNK, step, 0)
    share = share_ref[...]
    whole = share + pltpu.roll(share, LANES // 2, 1)
    first = lax.broadcasted_iota(jnp.int32, (depth // 2, LANES), 1) < LANES // 2
    for f in range(3):
        product = value_ref[f] * share
        ratio_ref[...] = (product + pltpu.roll(product, LANES // 2, 1)) / whole
        even = ratio_ref[pl.ds(0, depth // 2, stride=2), :]
        odd = ratio_ref[pl.ds(1, depth // 2, stride=2), :]
        regrid_ref[f] = jnp.where(first, even, odd)


def to_rows(source_ref, source_at, table_ref, table_at, count, name_at, unroll):
    def piece(c, _):
        here = pl.ds(pl.multiple_of(source_at + c * LANES, LANES), LANES)
        name = lax.broadcasted_iota(jnp.int32, (8, LANES), 1) + (name_at + c * LANES)
        kind = lax.broadcasted_iota(jnp.int32, (8, LANES), 0)
        name = jnp.where(kind < 6, name, jnp.where(kind == 6, 1, 0)).astype(jnp.float32)
        block = jnp.concatenate([source_ref[f, :, here] for f in range(3)] + [name], axis=0)
        there = pl.ds(pl.multiple_of(table_at + c * LANES, 8), LANES)
        table_ref[there, :KEEP] = jnp.transpose(block)
        return 0

    lax.fori_loop(0, count // LANES, piece, 0, unroll=unroll)


def walk(y_points, x_points, next_ref, first_ref, last_ref, visit, middle):
    def chain(c, _):
        base = pl.multiple_of(c * 16, 16)
        places = [first_ref[base + u] for u in range(16)]
        for x in range(x_points - 1):
            if x or not middle:
                visit(x, base, places)
            if x < x_points - 2:
                places = [next_ref[place] for place in places]
        if not middle:
            visit(x_points - 1, base, [last_ref[base + u] for u in range(16)])
        return 0

    lax.fori_loop(0, y_points // 16, chain, 0)


def start_kernel(
    n, x_points, y_points, state_hbm, rows_hbm, source_hbm, weight_hbm, metric_hbm, adjacent_hbm, edges_hbm, speed_hbm,
    state_ref, in_ref, regrid_ref, stepped_ref, west_ref, east_ref, table_ref, sum_ref, low_ref, high_ref, share_ref,
    rows_ref, metric_ref, source_ref, weight_ref, sea_source_ref, sea_weight_ref, sea_low_ref, sea_high_ref,
    sea_share_ref, value_ref, ratio_ref, pair_terms_ref, made_ref, surface_ref, terms_ref, out_ref, rim_ref, grid_ref,
    west_rim_ref, east_rim_ref, next_ref, first_ref, last_ref, speed_ref,
    load_sem, slot_send, slot_recv, edge_send, edge_recv, pair_send, pair_recv, made_send, made_recv,
):
    sec, dom = lax.axis_index("sec"), lax.axis_index("dom")
    right, left = lax.rem(dom + 1, n), lax.rem(dom + n - 1, n)
    mesh_ids = pl.DeviceIdType.MESH
    atmosphere, ocean = sec == 0, sec == 1
    load_state = pltpu.make_async_copy(state_hbm, state_ref, load_sem.at[0])
    load_rows = pltpu.make_async_copy(rows_hbm, rows_ref, load_sem.at[1])
    load_metric = pltpu.make_async_copy(metric_hbm, metric_ref, load_sem.at[2])
    load_next = pltpu.make_async_copy(adjacent_hbm.at[2], next_ref, load_sem.at[3])
    load_first = pltpu.make_async_copy(edges_hbm.at[0], first_ref, load_sem.at[4])
    load_last = pltpu.make_async_copy(edges_hbm.at[1], last_ref, load_sem.at[8])
    load_speed = pltpu.make_async_copy(speed_hbm, speed_ref, load_sem.at[5])
    load_source = pltpu.make_async_copy(source_hbm, source_ref, load_sem.at[6])
    load_weight = pltpu.make_async_copy(weight_hbm, weight_ref, load_sem.at[7])
    load_state.start()
    load_rows.start()
    barrier = pltpu.get_barrier_semaphore()

    def hello(a, b):
        pl.semaphore_signal(barrier, inc=1, device_id=(a, b), device_id_type=mesh_ids)

    @pl.when(atmosphere)
    def _():
        def greet(p, _):
            hello(1, p)

            @pl.when(p != dom)
            def _():
                hello(0, p)

            return 0

        lax.fori_loop(0, n, greet, 0)
        load_metric.start()
        load_speed.start()
        load_source.start()
        load_weight.start()

    @pl.when(ocean)
    def _():
        hello(0, dom)
        hello(1, left)
        hello(1, right)
        load_first.start()
        load_last.start()
        load_next.start()

    load_state.wait()
    depth, top, rows = state_ref.shape[2] // LANES, state_ref.shape[1] - 1, state_ref.shape[2]

    def column(x, u):
        return pl.ds(8 + (x + 1) * y_points + u, 1)

    def visit(x, base, places):
        found = [table_ref[pl.ds(place, 1), :] for place in places]
        for u in range(len(places)):
            grid_ref[column(x, base + u), :] = found[u]

    @pl.when(ocean)
    def _():
        to_rows(state_ref, 0, table_ref, 0, rows, 0, 8)
        load_first.wait()
        load_last.wait()

        def edge(c, _):
            base = pl.multiple_of(c * 16, 16)
            for listed, x in ((first_ref, 0), (last_ref, x_points - 1)):
                visit(x, base, [listed[base + u] for u in range(16)])
            return 0

        lax.fori_loop(0, y_points // 16, edge, 0)
        levels = top + 1
        for k, x in ((0, 0), (1, x_points - 1)):
            for c in range(y_points // LANES):
                at = 8 + (x + 1) * y_points + c * LANES
                block = jnp.transpose(grid_ref[at : at + LANES, :KEEP])
                for f in range(3):
                    rim_ref[f, :, k * y_points + c * LANES : k * y_points + (c + 1) * LANES] = block[
                        f * levels : (f + 1) * levels
                    ]

    for f in range(3):
        for h in range(depth):
            surface_ref[f * depth + h : f * depth + h + 1, :] = state_ref[
                f, top : top + 1, h * LANES : (h + 1) * LANES
            ]
    terms_ref[...] = two_terms(surface_ref[...])
    load_rows.wait()

    def remote(source, target, send, recv, device):
        return pltpu.make_async_remote_copy(
            src_ref=source, dst_ref=target, send_sem=send, recv_sem=recv, device_id=device, device_id_type=mesh_ids
        )

    lines = out_ref.shape[2]
    peers = CHUNK // lines
    chunks = rows_ref.shape[0] // CHUNK

    def slots(p):
        return remote(out_ref.at[p], in_ref.at[sec, dom], slot_send.at[p], slot_recv.at[sec, dom], (0, p))

    def own_slots():
        return pltpu.make_async_copy(out_ref.at[dom], in_ref.at[0, dom], slot_recv.at[0, dom])

    pair_source = remote(source_hbm, sea_source_ref, pair_send.at[0], pair_recv.at[0], (0, dom))
    pair_weight = remote(weight_hbm, sea_weight_ref, pair_send.at[1], pair_recv.at[1], (0, dom))
    made = remote(made_ref, regrid_ref, made_send, made_recv, (1, dom))

    def send(k, _):
        c = lax.rem(k + dom * chunks // n, chunks)
        index = row_of(rows_ref, c * CHUNK, CHUNK)
        values = pick(terms_ref[...], depth, index & (LANES - 1), index >> 7)
        for f in range(3):
            for r in range(CHUNK):
                out_ref[c * peers + r // lines, f, pl.ds(r % lines, 1), :] = values[f][:, r * LANES : (r + 1) * LANES]

        @pl.when(jnp.logical_and(k == 0, atmosphere))
        def _():
            pl.semaphore_wait(barrier, n)

        @pl.when(jnp.logical_and(k == 0, ocean))
        def _():
            pl.semaphore_wait(barrier, n + 2)
            pair_source.start()
            pair_weight.start()

        def ship(j, _):
            p = c * peers + j
            here = jnp.logical_and(atmosphere, p == dom)

            @pl.when(here)
            def _():
                own_slots().start()

            @pl.when(jnp.logical_not(here))
            def _():
                slots(p).start()

            return 0

        lax.fori_loop(0, peers, ship, 0)
        return 0

    lax.fori_loop(0, chunks, send, 0)

    first, last = pl.ds(0, y_points), pl.ds(rows - y_points, y_points)
    rim_first, rim_last = rim_ref.at[:, :, first], rim_ref.at[:, :, pl.ds(y_points, y_points)]
    air_edges = [
        remote(stepped_ref.at[:, :, last], west_ref, edge_send.at[0], edge_recv.at[0], (0, right)),
        remote(stepped_ref.at[:, :, first], east_ref, edge_send.at[1], edge_recv.at[1], (0, left)),
    ]
    sea_edges = [
        remote(rim_last, west_ref, edge_send.at[0], edge_recv.at[0], (1, right)),
        remote(rim_first, east_ref, edge_send.at[1], edge_recv.at[1], (1, left)),
    ]

    def sent(p, _):
        @pl.when(jnp.logical_not(jnp.logical_and(atmosphere, p == dom)))
        def _():
            slots(p).wait_send()

        return 0

    def arrival(a, p):
        remote(out_ref.at[p], in_ref.at[a, p], slot_send.at[p], slot_recv.at[a, p], (0, p)).wait_recv()

    @pl.when(atmosphere)
    def _():
        load_metric.wait()
        load_speed.wait()
        advance(x_points, y_points, state_ref, metric_ref, speed_ref, stepped_ref)
        for each in air_edges:
            each.start()
        load_source.wait()
        load_weight.wait()
        split_pairs(source_ref, weight_ref, low_ref, high_ref, share_ref)
        pair_source.wait_recv()
        pair_weight.wait_recv()
        split_pairs(sea_source_ref, sea_weight_ref, sea_low_ref, sea_high_ref, sea_share_ref)

        def from_air(p, _):
            @pl.when(p == dom)
            def _():
                own_slots().wait()

            @pl.when(p != dom)
            def _():
                arrival(0, p)

            return 0

        lax.fori_loop(0, n, from_air, 0)
        regrid_into(
            made_ref, lambda f: in_ref[0, :, f], sea_low_ref, sea_high_ref, sea_share_ref,
            pair_terms_ref, value_ref, ratio_ref,
        )
        made.start()

        def from_sea(p, _):
            arrival(1, p)
            return 0

        lax.fori_loop(0, n, from_sea, 0)
        for each in air_edges:
            each.wait()
        lax.fori_loop(0, n, sent, 0)
        made.wait_send()

    @pl.when(ocean)
    def _():
        for each in sea_edges:
            each.start()
        load_next.wait()
        walk(y_points, x_points, next_ref, first_ref, last_ref, visit, True)
        for each in sea_edges:
            each.wait()
        to_rows(west_ref, 0, west_rim_ref, 8, y_points, rows, 4)
        to_rows(east_ref, 0, east_rim_ref, 8, y_points, rows + y_points, 4)
        sum_neighbours(x_points, y_points, grid_ref, (west_rim_ref, east_rim_ref), sum_ref)
        pair_source.wait_send()
        pair_weight.wait_send()
        lax.fori_loop(0, n, sent, 0)
        made.wait_recv()


def sum_neighbours(x_points, y_points, grid_ref, rims, sum_ref):
    lane = lax.broadcasted_iota(jnp.int32, (8, LANES), 1)
    row = lax.broadcasted_iota(jnp.int32, (8, LANES), 0)

    def mask(*names):
        kept = lane < 24
        for name in names:
            kept = kept | (lane == 24 + name)
        return kept.astype(jnp.float32)

    same, tilted = mask(2, 3), mask(4, 5)
    above, below = mask(0), mask(1)
    east, west = mask(2, 4), mask(3, 5)

    def read(x, at, shift):
        if 0 <= x < x_points:
            return grid_ref[pl.ds(8 + (x + 1) * y_points + at + shift, 8), :]
        return rims[0 if x < 0 else 1][pl.ds(8 + at + shift, 8), :]

    def inner(c, _):
        at = c * 8
        joined = {}
        for x in range(-1, x_points + 1):
            tilt = -1 if x % 2 else 1
            joined[x] = read(x, at, 0) * same + read(x, at, tilt) * tilted
            if x > 0:
                upright = read(x - 1, at, 1) * above + read(x - 1, at, -1) * below
                total = upright + joined[x] * east + joined[x - 2] * west
                sum_ref[pl.ds(pl.multiple_of((x - 1) * y_points + at, 8), 8), :] = total
        return 0

    lax.fori_loop(1, y_points // 8 - 1, inner, 0)

    for at, gone, missing in ((0, row == 0, -1), (y_points - 8, row == 7, 1)):
        for x in range(x_points):
            own = read(x, at, 0)
            tilt = 1 if x % 2 else -1

            def near(x, shift):
                value = read(x, at, shift)
                return jnp.where(gone, own, value) if shift == missing else value

            total = near(x, 1) * above + near(x, -1) * below
            total = total + (near(x + 1, 0) * same + near(x + 1, tilt) * tilted) * east
            total = total + (near(x - 1, 0) * same + near(x - 1, tilt) * tilted) * west
            sum_ref[x * y_points + at : x * y_points + at + 8, :] = total


def end_kernel(
    x_points, y_points, state_ref, in_ref, made_ref, stepped_ref, west_ref, east_ref, table_in_ref, sum_ref,
    low_ref, high_ref, share_ref, kappa_hbm, adjacent_hbm, edges_hbm, rate_hbm,
    new_hbm, table_ref,
    new_ref, ratio_ref, value_ref, pair_terms_ref, regrid_ref, kappa_ref, adjacent_ref, next_ref, few_ref,
    every_ref, first_ref, last_ref, rate_ref, load_sem, store_sem,
):
    sec = lax.axis_index("sec")
    levels, rows = state_ref.shape[1], state_ref.shape[2]
    load_rate = pltpu.make_async_copy(rate_hbm, rate_ref, load_sem.at[0])
    load_next = pltpu.make_async_copy(adjacent_hbm.at[2], next_ref, load_sem.at[1])
    load_adjacent = pltpu.make_async_copy(adjacent_hbm, adjacent_ref, load_sem.at[2])
    load_kappa = pltpu.make_async_copy(kappa_hbm, kappa_ref, load_sem.at[3])
    load_first = pltpu.make_async_copy(edges_hbm.at[0], first_ref, load_sem.at[4])
    load_last = pltpu.make_async_copy(edges_hbm.at[1], last_ref, load_sem.at[6])
    load_rate.start()

    @pl.when(sec == 1)
    def _():
        load_first.start()
        load_last.start()
        load_next.start()
        load_adjacent.start()
        load_kappa.start()

    load_rate.wait()

    def couple(f, here, value, relaxed):
        row = lax.broadcasted_iota(jnp.int32, value.shape, 0)
        new_ref[f, :, here] = jnp.where(row == levels - 1, value + rate_ref[0, f] * (relaxed - value), value)

    @pl.when(sec == 0)
    def _():
        regrid_into(
            regrid_ref, lambda f: in_ref[1, :, f], low_ref, high_ref, share_ref, pair_terms_ref, value_ref, ratio_ref
        )
        stores = [pltpu.make_async_copy(new_ref.at[f], new_hbm.at[f], store_sem.at[f]) for f in range(3)]
        for f in range(3):
            for x in range(x_points):
                here = slice(x * y_points, (x + 1) * y_points)
                value = stepped_ref[f, :, here]
                if x % 4 == 3:
                    other = (
                        stepped_ref[f, :, (x + 1) * y_points : (x + 2) * y_points]
                        if x < x_points - 1
                        else east_ref[f]
                    )
                    value = (value + other) * 0.5
                elif x % 4 == 0:
                    other = stepped_ref[f, :, (x - 1) * y_points : x * y_points] if x else west_ref[f]
                    value = (value + other) * 0.5
                position = lax.broadcasted_iota(jnp.int32, value.shape, 1)
                phase = position % 4
                after = pltpu.roll(value, y_points - 1, 1)
                before = pltpu.roll(value, 1, 1)
                averaged = jnp.where(
                    (phase == 3) & (position < y_points - 1),
                    (value + after) * 0.5,
                    jnp.where((phase == 0) & (position > 0), (value + before) * 0.5, value),
                )
                lines = y_points // LANES
                relaxed = jnp.concatenate(
                    [regrid_ref[f, x * lines + i : x * lines + i + 1, :] for i in range(lines)], axis=1
                )
                couple(f, here, averaged, relaxed)
            stores[f].start()
        for each in stores:
            each.wait()

    @pl.when(sec == 1)
    def _():
        load_next.wait()
        load_first.wait()
        load_last.wait()

        def visit(x, base, places):
            found = [sum_ref[pl.ds(x * y_points + base + u, 1), :] for u in range(len(places))]
            for u, place in enumerate(places):
                table_ref[pl.ds(place, 1), :] = found[u]

        walk(y_points, x_points, next_ref, first_ref, last_ref, visit, False)
        load_adjacent.wait()
        load_kappa.wait()
        part = rows // 4
        stores = [
            pltpu.make_async_copy(
                new_ref.at[:, :, pl.ds(k * part, part)], new_hbm.at[:, :, pl.ds(k * part, part)], store_sem.at[k]
            )
            for k in range(4)
        ]

        def finish(c, wrong):
            here = pl.ds(pl.multiple_of(c * LANES, LANES), LANES)
            block = jnp.transpose(table_ref[here, :KEEP])
            kappa = kappa_ref[pl.ds(c, 1), :]
            for f in range(3):
                value = state_ref[f, :, here]
                swept = value + kappa * (block[f * levels : (f + 1) * levels] - 6.0 * value)
                couple(f, here, swept, made_ref[f, pl.ds(c, 1), :])
            named = adjacent_ref[:, here].astype(jnp.float32)
            names = block[24:32]
            off = (names[0:6] != named).astype(jnp.float32)
            return jnp.maximum(wrong, jnp.maximum(jnp.max(off, axis=0, keepdims=True), names[6:7]))

        wrong = jnp.zeros((1, LANES), jnp.float32)
        for k in range(4):
            blocks = part // LANES
            wrong = lax.fori_loop(k * blocks, (k + 1) * blocks, finish, wrong, unroll=8)
            stores[k].start()
        for each in stores:
            each.wait()

        @pl.when(jnp.max(wrong) > 0.0)
        def _():
            to_rows(state_ref, 0, every_ref, 0, rows, 0, 1)
            to_rows(west_ref, 0, every_ref, rows, y_points, rows, 1)
            to_rows(east_ref, 0, every_ref, rows + y_points, y_points, rows + y_points, 1)

            def block(c, _):
                fetch = pltpu.make_async_copy(
                    adjacent_hbm.at[:, pl.ds(pl.multiple_of(c * LANES, LANES), LANES)], few_ref, load_sem.at[5]
                )
                fetch.start()
                fetch.wait()

                def cell(i, _):
                    total = every_ref[pl.ds(few_ref[0, i], 1), :]
                    for j in range(1, 6):
                        total = total + every_ref[pl.ds(few_ref[j, i], 1), :]
                    table_ref[pl.ds(c * LANES + i, 1), :] = total
                    return 0

                lax.fori_loop(0, LANES, cell, 0)
                return 0

            lax.fori_loop(0, rows // LANES, block, 0)
            lax.fori_loop(0, rows // LANES, finish, wrong)
            whole = pltpu.make_async_copy(new_ref, new_hbm, store_sem.at[0])
            whole.start()
            whole.wait()


def body(
    state, send_rows, intersection_source, intersection_weight, couple_rate, atm_metric, wave_speed,
    ocean_adjacent, ocean_edges, ocean_kappa,
):
    levels, rows = state.shape[1], state.shape[2]
    y_points = ocean_edges.shape[1]
    x_points = rows // y_points
    n = lax.axis_size("dom")
    slots = send_rows.shape[0]
    lines = slots // n // LANES
    f32, i32 = jnp.float32, jnp.int32
    pairs = slots // LANES
    source, weight = intersection_source.reshape(-1, LANES), intersection_weight.reshape(-1, LANES)
    placed, slot_rows, source, weight, metric, adjacent, kappa, edges, speed, rate = [
        pltpu.with_memory_space_constraint(each, pltpu.HBM)
        for each in (
            state, send_rows.reshape(-1, LANES), source, weight, atm_metric, ocean_adjacent,
            ocean_kappa.reshape(-1, LANES), ocean_edges, wave_speed, couple_rate,
        )
    ]

    border = jax.ShapeDtypeStruct((3, levels, y_points), f32)
    whole = jax.ShapeDtypeStruct(state.shape, f32)
    table = jax.ShapeDtypeStruct((rows, LANES), f32)
    index, share = jax.ShapeDtypeStruct((pairs, LANES), i32), jax.ShapeDtypeStruct((pairs, LANES), f32)
    arriving = jax.ShapeDtypeStruct((2, n, 3, lines, LANES), f32)
    made = jax.ShapeDtypeStruct((3, rows // LANES, LANES), f32)
    dma = pltpu.SemaphoreType.DMA
    held = pl.pallas_call(
        functools.partial(start_kernel, n, x_points, y_points),
        out_shape=[whole, arriving, made, whole, border, border, table, table, index, index, share],
        in_specs=[HBM] * 8,
        out_specs=[VMEM] * 11,
        scratch_shapes=[
            pltpu.VMEM((pairs, LANES), i32),
            pltpu.VMEM(atm_metric.shape, f32),
            pltpu.VMEM((pairs, LANES), i32),
            pltpu.VMEM((pairs, LANES), f32),
            pltpu.VMEM((pairs, LANES), i32),
            pltpu.VMEM((pairs, LANES), f32),
            pltpu.VMEM((pairs, LANES), i32),
            pltpu.VMEM((pairs, LANES), i32),
            pltpu.VMEM((pairs, LANES), f32),
            pltpu.VMEM((3, pairs, LANES), f32),
            pltpu.VMEM((pairs, LANES), f32),
            pltpu.VMEM((3 * pairs, 2 * LANES), jnp.bfloat16),
            pltpu.VMEM(made.shape, f32),
            pltpu.VMEM((3 * rows // LANES, LANES), f32),
            pltpu.VMEM((3 * rows // LANES, 2 * LANES), jnp.bfloat16),
            pltpu.VMEM(arriving.shape[1:], f32),
            pltpu.VMEM((3, levels, 2 * y_points), f32),
            pltpu.VMEM(((x_points + 2) * y_points + 16, LANES), f32),
            pltpu.VMEM((y_points + 16, LANES), f32),
            pltpu.VMEM((y_points + 16, LANES), f32),
            pltpu.SMEM((rows,), i32),
            pltpu.SMEM((y_points,), i32),
            pltpu.SMEM((y_points,), i32),
            pltpu.SMEM(wave_speed.shape, f32),
            dma((9,)),
            dma((n,)),
            dma((2, n)),
            dma((2,)),
            dma((2,)),
            dma((2,)),
            dma((2,)),
            dma,
            dma,
        ],
        compiler_params=pltpu.CompilerParams(collective_id=0, has_side_effects=True, **PARAMS),
        name="start",
    )(placed, slot_rows, source, weight, metric, adjacent, edges, speed)

    new_state, _ = pl.pallas_call(
        functools.partial(end_kernel, x_points, y_points),
        out_shape=[whole, table],
        in_specs=[VMEM] * 11 + [HBM] * 4,
        out_specs=[HBM, VMEM],
        input_output_aliases={6: 1},
        scratch_shapes=[
            pltpu.VMEM(state.shape, f32),
            pltpu.VMEM((pairs, LANES), f32),
            pltpu.VMEM((3, pairs, LANES), f32),
            pltpu.VMEM((3 * pairs, 2 * LANES), jnp.bfloat16),
            pltpu.VMEM((3, rows // LANES, LANES), f32),
            pltpu.VMEM((rows // LANES, LANES), f32),
            pltpu.VMEM(ocean_adjacent.shape, i32),
            pltpu.SMEM((rows,), i32),
            pltpu.SMEM((6, LANES), i32),
            pltpu.VMEM((rows + 2 * y_points, LANES), f32),
            pltpu.SMEM((y_points,), i32),
            pltpu.SMEM((y_points,), i32),
            pltpu.SMEM(couple_rate.shape, f32),
            dma((7,)),
            dma((4,)),
        ],
        compiler_params=pltpu.CompilerParams(**PARAMS),
        name="end",
    )(*held, kappa, adjacent, edges, rate)
    return new_state


def solution(mesh):
    in_specs = (
        P(None, None, ("sec", "dom")),
        P(("sec", "dom")),
        P(("sec", "dom")),
        P(("sec", "dom")),
        P("sec", None),
        P(None, "dom"),
        P(),
        P(None, "dom"),
        P(None, "dom"),
        P("dom"),
    )
    out_specs = P(None, None, ("sec", "dom"))
    return jax.shard_map(body, mesh=mesh, in_specs=in_specs, out_specs=out_specs, check_vma=False)
```

```python
import functools
import jax
import jax.numpy as jnp
import numpy as np
from jax import lax
from jax.experimental import pallas as pl
from jax.experimental.pallas import tpu as pltpu
from jax.sharding import PartitionSpec as P

TIME_STEP = 0.05
LANES = 128
VMEM = pl.BlockSpec(memory_space=pltpu.VMEM)
SMEM = pl.BlockSpec(memory_space=pltpu.SMEM)
HBM = pl.BlockSpec(memory_space=pltpu.HBM)
PARAMS = dict(vmem_limit_bytes=24 << 20)


def gll_derivative():
    nodes = np.array([-1.0, -1.0 / np.sqrt(5.0), 1.0 / np.sqrt(5.0), 1.0])
    barycentric = np.array(
        [1.0 / np.prod([nodes[i] - nodes[j] for j in range(4) if j != i]) for i in range(4)]
    )
    matrix = np.zeros((4, 4))
    for i in range(4):
        for j in range(4):
            if i != j:
                matrix[i, j] = barycentric[j] / barycentric[i] / (nodes[i] - nodes[j])
        matrix[i, i] = -np.sum(matrix[i])
    return matrix


DERIVATIVE = gll_derivative()


def lane_phase(shape):
    return lax.broadcasted_iota(jnp.int32, shape, 1) % 4


def along_second(value, phase):
    width = value.shape[1]
    total = jnp.zeros_like(value)
    for shift in range(-3, 4):
        factor = jnp.zeros(value.shape, jnp.float32)
        for i in range(4):
            if 0 <= i + shift < 4:
                factor = jnp.where(phase == i, np.float32(DERIVATIVE[i, i + shift]), factor)
        moved = value if shift == 0 else pltpu.roll(value, (-shift) % width, 1)
        total = total + factor * moved
    return total


def advance(x_points, y_points, state_ref, metric_ref, speed_ref, stepped_ref):
    level = lax.broadcasted_iota(jnp.int32, (state_ref.shape[1], LANES), 0)
    speed = jnp.zeros(level.shape, jnp.float32)
    for k in range(level.shape[0]):
        speed = jnp.where(level == k, speed_ref[k], speed)

    def piece(g, _):
        def at(i, f):
            return state_ref[f, :, pl.ds(pl.multiple_of(start + i * y_points, LANES), LANES)]

        start = (g // (y_points // LANES)) * 4 * y_points + (g % (y_points // LANES)) * LANES
        phase = lane_phase((state_ref.shape[1], LANES))
        u = [at(i, 0) for i in range(4)]
        v = [at(i, 1) for i in range(4)]
        h = [at(i, 2) for i in range(4)]
        for i in range(4):
            here = pl.ds(pl.multiple_of(start + i * y_points, LANES), LANES)
            gx = metric_ref[0:1, here]
            gy = metric_ref[1:2, here]
            dx_h = sum(np.float32(DERIVATIVE[i, j]) * h[j] for j in range(4))
            dx_u = sum(np.float32(DERIVATIVE[i, j]) * u[j] for j in range(4))
            stepped_ref[0, :, here] = u[i] - TIME_STEP * (gx * dx_h)
            stepped_ref[1, :, here] = v[i] - TIME_STEP * (gy * along_second(h[i], phase))
            spread = gx * dx_u + gy * along_second(v[i], phase)
            stepped_ref[2, :, here] = h[i] - TIME_STEP * speed * spread
        return 0

    lax.fori_loop(0, x_points // 4 * (y_points // LANES), piece, 0)


CHUNK = 32
KEEP = 32


def two_terms(table):
    high = table.astype(jnp.bfloat16)
    low = (table - high.astype(jnp.float32)).astype(jnp.bfloat16)
    return jnp.concatenate([high, low], axis=1)


def pick(terms, depth, low, high):
    count = low.shape[1]
    low = jnp.broadcast_to(low.astype(jnp.int16), (LANES, count))
    lane = lax.broadcasted_iota(jnp.int16, (LANES, LANES), 0)
    lane = jnp.concatenate([lane] * (count // LANES), axis=1)
    hot = jnp.where(lane == low, jnp.bfloat16(1), jnp.bfloat16(0))
    found = jnp.dot(terms, jnp.concatenate([hot, hot], axis=0), preferred_element_type=jnp.float32)
    high = jnp.broadcast_to(high, (8, count))
    own = lax.broadcasted_iota(jnp.int32, high.shape, 0) == (high & 7)
    picked = []
    for f in range(3):
        parts = [found[f * depth + 8 * i : f * depth + 8 * i + 8] for i in range(depth // 8)]
        bit = 3
        while len(parts) > 1:
            odd = ((high >> bit) & 1) == 1
            parts = [jnp.where(odd, parts[i + 1], parts[i]) for i in range(0, len(parts), 2)]
            bit += 1
        picked.append(jnp.sum(jnp.where(own, parts[0], 0.0), axis=0, keepdims=True))
    return picked


def row_of(ref, start, count):
    return jnp.concatenate([ref[pl.ds(start + r, 1), :] for r in range(count)], axis=1)


def split_pairs(source_ref, weight_ref, low_ref, high_ref, share_ref):
    i = lax.broadcasted_iota(jnp.int32, (LANES, LANES), 0)
    j = lax.broadcasted_iota(jnp.int32, (LANES, LANES), 1)
    half = LANES // 2
    chosen = (i == 2 * (j % half) + j // half).astype(jnp.float32).astype(jnp.bfloat16)

    def move(value):
        return jnp.dot(value.astype(jnp.bfloat16), chosen, preferred_element_type=jnp.float32)

    source = source_ref[...]
    low_ref[...] = (move((source & (LANES - 1)).astype(jnp.float32)) + 0.5).astype(jnp.int32)
    high_ref[...] = (move((source >> 7).astype(jnp.float32)) + 0.5).astype(jnp.int32)
    weight = weight_ref[...]
    upper = weight.astype(jnp.bfloat16).astype(jnp.float32)
    share_ref[...] = move(upper) + move(weight - upper)


def regrid_into(regrid_ref, arrived, low_ref, high_ref, share_ref, terms_ref, value_ref, ratio_ref):
    depth = low_ref.shape[0]
    for f in range(3):
        terms_ref[f * depth : (f + 1) * depth, :] = two_terms(arrived(f).reshape(depth, LANES))

    def step(c, _):
        low, high = row_of(low_ref, c * CHUNK, CHUNK), row_of(high_ref, c * CHUNK, CHUNK)
        values = pick(terms_ref[...], depth, low, high)
        for f in range(3):
            for r in range(CHUNK):
                value_ref[f, pl.ds(c * CHUNK + r, 1), :] = values[f][:, r * LANES : (r + 1) * LANES]
        return 0

    lax.fori_loop(0, depth // CHUNK, step, 0)
    share = share_ref[...]
    whole = share + pltpu.roll(share, LANES // 2, 1)
    first = lax.broadcasted_iota(jnp.int32, (depth // 2, LANES), 1) < LANES // 2
    for f in range(3):
        product = value_ref[f] * share
        ratio_ref[...] = (product + pltpu.roll(product, LANES // 2, 1)) / whole
        even = ratio_ref[pl.ds(0, depth // 2, stride=2), :]
        odd = ratio_ref[pl.ds(1, depth // 2, stride=2), :]
        regrid_ref[f] = jnp.where(first, even, odd)


def to_rows(source_ref, source_at, table_ref, table_at, count, name_at, unroll):
    def piece(c, _):
        here = pl.ds(pl.multiple_of(source_at + c * LANES, LANES), LANES)
        name = lax.broadcasted_iota(jnp.int32, (8, LANES), 1) + (name_at + c * LANES)
        kind = lax.broadcasted_iota(jnp.int32, (8, LANES), 0)
        name = jnp.where(kind < 6, name, jnp.where(kind == 6, 1, 0)).astype(jnp.float32)
        block = jnp.concatenate([source_ref[f, :, here] for f in range(3)] + [name], axis=0)
        there = pl.ds(pl.multiple_of(table_at + c * LANES, 8), LANES)
        table_ref[there, :KEEP] = jnp.transpose(block)
        return 0

    lax.fori_loop(0, count // LANES, piece, 0, unroll=unroll)


def walk(y_points, x_points, next_ref, first_ref, last_ref, visit, middle):
    def chain(c, _):
        base = pl.multiple_of(c * 8, 8)
        places = [first_ref[base + u] for u in range(8)]
        for x in range(x_points - 1):
            if x or not middle:
                visit(x, base, places)
            if x < x_points - 2:
                places = [next_ref[place] for place in places]
        if not middle:
            visit(x_points - 1, base, [last_ref[base + u] for u in range(8)])
        return 0

    lax.fori_loop(0, y_points // 8, chain, 0)


def start_kernel(
    n, x_points, y_points, state_hbm, rows_hbm, source_hbm, weight_hbm, metric_hbm, adjacent_hbm, edges_hbm, speed_hbm,
    state_ref, in_ref, regrid_ref, stepped_ref, west_ref, east_ref, table_ref, sum_ref, low_ref, high_ref, share_ref,
    rows_ref, metric_ref, source_ref, weight_ref, sea_source_ref, sea_weight_ref, sea_low_ref, sea_high_ref,
    sea_share_ref, value_ref, ratio_ref, pair_terms_ref, made_ref, surface_ref, terms_ref, out_ref, rim_ref, grid_ref,
    west_rim_ref, east_rim_ref, next_ref, first_ref, last_ref, speed_ref,
    load_sem, slot_send, slot_recv, edge_send, edge_recv, pair_send, pair_recv, made_send, made_recv,
):
    sec, dom = lax.axis_index("sec"), lax.axis_index("dom")
    right, left = lax.rem(dom + 1, n), lax.rem(dom + n - 1, n)
    mesh_ids = pl.DeviceIdType.MESH
    atmosphere, ocean = sec == 0, sec == 1
    load_state = pltpu.make_async_copy(state_hbm, state_ref, load_sem.at[0])
    load_rows = pltpu.make_async_copy(rows_hbm, rows_ref, load_sem.at[1])
    load_metric = pltpu.make_async_copy(metric_hbm, metric_ref, load_sem.at[2])
    load_next = pltpu.make_async_copy(adjacent_hbm.at[2], next_ref, load_sem.at[3])
    load_first = pltpu.make_async_copy(edges_hbm.at[0], first_ref, load_sem.at[4])
    load_last = pltpu.make_async_copy(edges_hbm.at[1], last_ref, load_sem.at[8])
    load_speed = pltpu.make_async_copy(speed_hbm, speed_ref, load_sem.at[5])
    load_source = pltpu.make_async_copy(source_hbm, source_ref, load_sem.at[6])
    load_weight = pltpu.make_async_copy(weight_hbm, weight_ref, load_sem.at[7])
    load_state.start()
    load_rows.start()
    barrier = pltpu.get_barrier_semaphore()

    def hello(a, b):
        pl.semaphore_signal(barrier, inc=1, device_id=(a, b), device_id_type=mesh_ids)

    @pl.when(atmosphere)
    def _():
        def greet(p, _):
            hello(1, p)

            @pl.when(p != dom)
            def _():
                hello(0, p)

            return 0

        lax.fori_loop(0, n, greet, 0)
        load_metric.start()
        load_speed.start()
        load_source.start()
        load_weight.start()

    @pl.when(ocean)
    def _():
        hello(0, dom)
        hello(1, left)
        hello(1, right)
        load_first.start()
        load_last.start()
        load_next.start()

    load_state.wait()
    depth, top, rows = state_ref.shape[2] // LANES, state_ref.shape[1] - 1, state_ref.shape[2]

    def visit(x, base, places):
        found = [table_ref[pl.ds(place, 1), :] for place in places]
        for u in range(len(places)):
            grid_ref[pl.ds(base + (8 + (x + 1) * y_points + u), 1), :] = found[u]

    @pl.when(ocean)
    def _():
        to_rows(state_ref, 0, table_ref, 0, rows, 0, 8)
        load_first.wait()
        load_last.wait()

        def edge(c, _):
            base = pl.multiple_of(c * 8, 8)
            for listed, x in ((first_ref, 0), (last_ref, x_points - 1)):
                visit(x, base, [listed[base + u] for u in range(8)])
            return 0

        lax.fori_loop(0, y_points // 8, edge, 0)
        levels = top + 1
        for k, x in ((0, 0), (1, x_points - 1)):
            for c in range(y_points // LANES):
                at = 8 + (x + 1) * y_points + c * LANES
                block = jnp.transpose(grid_ref[at : at + LANES, :KEEP])
                for f in range(3):
                    rim_ref[f, :, k * y_points + c * LANES : k * y_points + (c + 1) * LANES] = block[
                        f * levels : (f + 1) * levels
                    ]

    for f in range(3):
        for h in range(depth):
            surface_ref[f * depth + h : f * depth + h + 1, :] = state_ref[
                f, top : top + 1, h * LANES : (h + 1) * LANES
            ]
    terms_ref[...] = two_terms(surface_ref[...])
    load_rows.wait()

    def remote(source, target, send, recv, device):
        return pltpu.make_async_remote_copy(
            src_ref=source, dst_ref=target, send_sem=send, recv_sem=recv, device_id=device, device_id_type=mesh_ids
        )

    lines = out_ref.shape[2]
    peers = CHUNK // lines
    chunks = rows_ref.shape[0] // CHUNK

    def slots(p):
        return remote(out_ref.at[p], in_ref.at[sec, dom], slot_send.at[p], slot_recv.at[sec, dom], (0, p))

    def own_slots():
        return pltpu.make_async_copy(out_ref.at[dom], in_ref.at[0, dom], slot_recv.at[0, dom])

    pair_source = remote(source_hbm, sea_source_ref, pair_send.at[0], pair_recv.at[0], (0, dom))
    pair_weight = remote(weight_hbm, sea_weight_ref, pair_send.at[1], pair_recv.at[1], (0, dom))
    made = remote(made_ref, regrid_ref, made_send, made_recv, (1, dom))

    first, last = pl.ds(0, y_points), pl.ds(rows - y_points, y_points)
    rim_first, rim_last = rim_ref.at[:, :, first], rim_ref.at[:, :, pl.ds(y_points, y_points)]
    air_edges = [
        remote(stepped_ref.at[:, :, last], west_ref, edge_send.at[0], edge_recv.at[0], (0, right)),
        remote(stepped_ref.at[:, :, first], east_ref, edge_send.at[1], edge_recv.at[1], (0, left)),
    ]
    sea_edges = [
        remote(rim_last, west_ref, edge_send.at[0], edge_recv.at[0], (1, right)),
        remote(rim_first, east_ref, edge_send.at[1], edge_recv.at[1], (1, left)),
    ]

    def send(k, _):
        c = lax.rem(k + dom * chunks // n, chunks)
        index = row_of(rows_ref, c * CHUNK, CHUNK)
        values = pick(terms_ref[...], depth, index & (LANES - 1), index >> 7)
        for f in range(3):
            for r in range(CHUNK):
                out_ref[c * peers + r // lines, f, pl.ds(r % lines, 1), :] = values[f][:, r * LANES : (r + 1) * LANES]

        @pl.when(jnp.logical_and(k == 0, atmosphere))
        def _():
            pl.semaphore_wait(barrier, n)

        @pl.when(jnp.logical_and(k == 0, ocean))
        def _():
            pl.semaphore_wait(barrier, n + 2)
            for each in sea_edges:
                each.start()
            pair_source.start()
            pair_weight.start()

        def ship(j, _):
            p = c * peers + j
            here = jnp.logical_and(atmosphere, p == dom)

            @pl.when(here)
            def _():
                own_slots().start()

            @pl.when(jnp.logical_not(here))
            def _():
                slots(p).start()

            return 0

        lax.fori_loop(0, peers, ship, 0)
        return 0

    lax.fori_loop(0, chunks, send, 0)

    def sent(p, _):
        @pl.when(jnp.logical_not(jnp.logical_and(atmosphere, p == dom)))
        def _():
            slots(p).wait_send()

        return 0

    def arrival(a, p):
        remote(out_ref.at[p], in_ref.at[a, p], slot_send.at[p], slot_recv.at[a, p], (0, p)).wait_recv()

    @pl.when(atmosphere)
    def _():
        load_metric.wait()
        load_speed.wait()
        advance(x_points, y_points, state_ref, metric_ref, speed_ref, stepped_ref)
        for each in air_edges:
            each.start()
        load_source.wait()
        load_weight.wait()
        split_pairs(source_ref, weight_ref, low_ref, high_ref, share_ref)
        pair_source.wait_recv()
        pair_weight.wait_recv()
        split_pairs(sea_source_ref, sea_weight_ref, sea_low_ref, sea_high_ref, sea_share_ref)

        def from_air(p, _):
            @pl.when(p == dom)
            def _():
                own_slots().wait()

            @pl.when(p != dom)
            def _():
                arrival(0, p)

            return 0

        lax.fori_loop(0, n, from_air, 0)
        regrid_into(
            made_ref, lambda f: in_ref[0, :, f], sea_low_ref, sea_high_ref, sea_share_ref,
            pair_terms_ref, value_ref, ratio_ref,
        )
        made.start()

        def from_sea(p, _):
            arrival(1, p)
            return 0

        lax.fori_loop(0, n, from_sea, 0)
        for each in air_edges:
            each.wait()
        lax.fori_loop(0, n, sent, 0)
        made.wait_send()

    @pl.when(ocean)
    def _():
        load_next.wait()
        walk(y_points, x_points, next_ref, first_ref, last_ref, visit, True)
        rims = (west_rim_ref, east_rim_ref)
        sum_neighbours(x_points, y_points, grid_ref, rims, sum_ref, [range(1, x_points - 1)])
        for each in sea_edges:
            each.wait()
        to_rows(west_ref, 0, west_rim_ref, 8, y_points, rows, 4)
        to_rows(east_ref, 0, east_rim_ref, 8, y_points, rows + y_points, 4)
        sum_neighbours(x_points, y_points, grid_ref, rims, sum_ref, [range(1), range(x_points - 1, x_points)])
        pair_source.wait_send()
        pair_weight.wait_send()
        lax.fori_loop(0, n, sent, 0)
        made.wait_recv()


def sum_neighbours(x_points, y_points, grid_ref, rims, sum_ref, spans):
    lane = lax.broadcasted_iota(jnp.int32, (8, LANES), 1)
    row = lax.broadcasted_iota(jnp.int32, (8, LANES), 0)

    def mask(*names):
        kept = lane < 24
        for name in names:
            kept = kept | (lane == 24 + name)
        return kept.astype(jnp.float32)

    same, tilted = mask(2, 3), mask(4, 5)
    above, below = mask(0), mask(1)
    east, west = mask(2, 4), mask(3, 5)

    def read(x, at, shift):
        if 0 <= x < x_points:
            return grid_ref[pl.ds(at + (8 + (x + 1) * y_points + shift), 8), :]
        return rims[0 if x < 0 else 1][pl.ds(at + (8 + shift), 8), :]

    def inner(c, _):
        at = c * 8
        for span in spans:
            joined, upright = {}, {}
            for x in range(span.start - 1, span.stop + 1):
                middle, up, down = read(x, at, 0), read(x, at, 1), read(x, at, -1)
                joined[x] = middle * same + (down if x % 2 else up) * tilted
                upright[x] = up * above + down * below
                if x > span.start:
                    total = upright[x - 1] + joined[x] * east + joined[x - 2] * west
                    sum_ref[pl.ds(pl.multiple_of(at + (x - 1) * y_points, 8), 8), :] = total
        return 0

    lax.fori_loop(1, y_points // 8 - 1, inner, 0)

    for at, gone, missing in ((0, row == 0, -1), (y_points - 8, row == 7, 1)):
        for x in [x for span in spans for x in span]:
            own = read(x, at, 0)
            tilt = 1 if x % 2 else -1

            def near(x, shift):
                value = read(x, at, shift)
                return jnp.where(gone, own, value) if shift == missing else value

            total = near(x, 1) * above + near(x, -1) * below
            total = total + (near(x + 1, 0) * same + near(x + 1, tilt) * tilted) * east
            total = total + (near(x - 1, 0) * same + near(x - 1, tilt) * tilted) * west
            sum_ref[x * y_points + at : x * y_points + at + 8, :] = total


def end_kernel(
    x_points, y_points, state_ref, in_ref, made_ref, stepped_ref, west_ref, east_ref, table_in_ref, sum_ref,
    low_ref, high_ref, share_ref, kappa_hbm, adjacent_hbm, edges_hbm, rate_hbm,
    new_hbm, table_ref,
    new_ref, ratio_ref, value_ref, pair_terms_ref, regrid_ref, kappa_ref, adjacent_ref, next_ref, few_ref,
    every_ref, first_ref, last_ref, rate_ref, load_sem, store_sem,
):
    sec = lax.axis_index("sec")
    levels, rows = state_ref.shape[1], state_ref.shape[2]
    load_rate = pltpu.make_async_copy(rate_hbm, rate_ref, load_sem.at[0])
    load_next = pltpu.make_async_copy(adjacent_hbm.at[2], next_ref, load_sem.at[1])
    load_adjacent = pltpu.make_async_copy(adjacent_hbm, adjacent_ref, load_sem.at[2])
    load_kappa = pltpu.make_async_copy(kappa_hbm, kappa_ref, load_sem.at[3])
    load_first = pltpu.make_async_copy(edges_hbm.at[0], first_ref, load_sem.at[4])
    load_last = pltpu.make_async_copy(edges_hbm.at[1], last_ref, load_sem.at[6])
    load_rate.start()

    @pl.when(sec == 1)
    def _():
        load_first.start()
        load_last.start()
        load_next.start()
        load_adjacent.start()
        load_kappa.start()

    load_rate.wait()

    def couple(f, here, value, relaxed):
        row = lax.broadcasted_iota(jnp.int32, value.shape, 0)
        new_ref[f, :, here] = jnp.where(row == levels - 1, value + rate_ref[0, f] * (relaxed - value), value)

    @pl.when(sec == 0)
    def _():
        regrid_into(
            regrid_ref, lambda f: in_ref[1, :, f], low_ref, high_ref, share_ref, pair_terms_ref, value_ref, ratio_ref
        )
        stores = [pltpu.make_async_copy(new_ref.at[f], new_hbm.at[f], store_sem.at[f]) for f in range(3)]
        for f in range(3):
            for x in range(x_points):
                here = slice(x * y_points, (x + 1) * y_points)
                value = stepped_ref[f, :, here]
                if x % 4 == 3:
                    other = (
                        stepped_ref[f, :, (x + 1) * y_points : (x + 2) * y_points]
                        if x < x_points - 1
                        else east_ref[f]
                    )
                    value = (value + other) * 0.5
                elif x % 4 == 0:
                    other = stepped_ref[f, :, (x - 1) * y_points : x * y_points] if x else west_ref[f]
                    value = (value + other) * 0.5
                position = lax.broadcasted_iota(jnp.int32, value.shape, 1)
                phase = position % 4
                after = pltpu.roll(value, y_points - 1, 1)
                before = pltpu.roll(value, 1, 1)
                averaged = jnp.where(
                    (phase == 3) & (position < y_points - 1),
                    (value + after) * 0.5,
                    jnp.where((phase == 0) & (position > 0), (value + before) * 0.5, value),
                )
                lines = y_points // LANES
                relaxed = jnp.concatenate(
                    [regrid_ref[f, x * lines + i : x * lines + i + 1, :] for i in range(lines)], axis=1
                )
                couple(f, here, averaged, relaxed)
            stores[f].start()
        for each in stores:
            each.wait()

    @pl.when(sec == 1)
    def _():
        load_next.wait()
        load_first.wait()
        load_last.wait()

        def visit(x, base, places):
            found = [sum_ref[pl.ds(base + (x * y_points + u), 1), :] for u in range(len(places))]
            for u, place in enumerate(places):
                table_ref[pl.ds(place, 1), :] = found[u]

        walk(y_points, x_points, next_ref, first_ref, last_ref, visit, False)
        load_adjacent.wait()
        load_kappa.wait()
        part = rows // 4
        stores = [
            pltpu.make_async_copy(
                new_ref.at[:, :, pl.ds(k * part, part)], new_hbm.at[:, :, pl.ds(k * part, part)], store_sem.at[k]
            )
            for k in range(4)
        ]

        def finish(c, wrong):
            here = pl.ds(pl.multiple_of(c * LANES, LANES), LANES)
            block = jnp.transpose(table_ref[here, :KEEP])
            kappa = kappa_ref[pl.ds(c, 1), :]
            for f in range(3):
                value = state_ref[f, :, here]
                swept = value + kappa * (block[f * levels : (f + 1) * levels] - 6.0 * value)
                couple(f, here, swept, made_ref[f, pl.ds(c, 1), :])
            named = adjacent_ref[:, here].astype(jnp.float32)
            names = block[24:32]
            off = (names[0:6] != named).astype(jnp.float32)
            return jnp.maximum(wrong, jnp.maximum(jnp.max(off, axis=0, keepdims=True), names[6:7]))

        wrong = jnp.zeros((1, LANES), jnp.float32)
        for k in range(4):
            blocks = part // LANES
            wrong = lax.fori_loop(k * blocks, (k + 1) * blocks, finish, wrong, unroll=8)
            stores[k].start()
        for each in stores:
            each.wait()

        @pl.when(jnp.max(wrong) > 0.0)
        def _():
            to_rows(state_ref, 0, every_ref, 0, rows, 0, 1)
            to_rows(west_ref, 0, every_ref, rows, y_points, rows, 1)
            to_rows(east_ref, 0, every_ref, rows + y_points, y_points, rows + y_points, 1)

            def block(c, _):
                fetch = pltpu.make_async_copy(
                    adjacent_hbm.at[:, pl.ds(pl.multiple_of(c * LANES, LANES), LANES)], few_ref, load_sem.at[5]
                )
                fetch.start()
                fetch.wait()

                def cell(i, _):
                    total = every_ref[pl.ds(few_ref[0, i], 1), :]
                    for j in range(1, 6):
                        total = total + every_ref[pl.ds(few_ref[j, i], 1), :]
                    table_ref[pl.ds(c * LANES + i, 1), :] = total
                    return 0

                lax.fori_loop(0, LANES, cell, 0)
                return 0

            lax.fori_loop(0, rows // LANES, block, 0)
            lax.fori_loop(0, rows // LANES, finish, wrong)
            whole = pltpu.make_async_copy(new_ref, new_hbm, store_sem.at[0])
            whole.start()
            whole.wait()


def body(
    state, send_rows, intersection_source, intersection_weight, couple_rate, atm_metric, wave_speed,
    ocean_adjacent, ocean_edges, ocean_kappa,
):
    levels, rows = state.shape[1], state.shape[2]
    y_points = ocean_edges.shape[1]
    x_points = rows // y_points
    n = lax.axis_size("dom")
    slots = send_rows.shape[0]
    lines = slots // n // LANES
    f32, i32 = jnp.float32, jnp.int32
    pairs = slots // LANES
    source, weight = intersection_source.reshape(-1, LANES), intersection_weight.reshape(-1, LANES)
    placed, slot_rows, source, weight, metric, adjacent, kappa, edges, speed, rate = [
        pltpu.with_memory_space_constraint(each, pltpu.HBM)
        for each in (
            state, send_rows.reshape(-1, LANES), source, weight, atm_metric, ocean_adjacent,
            ocean_kappa.reshape(-1, LANES), ocean_edges, wave_speed, couple_rate,
        )
    ]

    border = jax.ShapeDtypeStruct((3, levels, y_points), f32)
    whole = jax.ShapeDtypeStruct(state.shape, f32)
    table = jax.ShapeDtypeStruct((rows, LANES), f32)
    index, share = jax.ShapeDtypeStruct((pairs, LANES), i32), jax.ShapeDtypeStruct((pairs, LANES), f32)
    arriving = jax.ShapeDtypeStruct((2, n, 3, lines, LANES), f32)
    made = jax.ShapeDtypeStruct((3, rows // LANES, LANES), f32)
    dma = pltpu.SemaphoreType.DMA
    held = pl.pallas_call(
        functools.partial(start_kernel, n, x_points, y_points),
        out_shape=[whole, arriving, made, whole, border, border, table, table, index, index, share],
        in_specs=[HBM] * 8,
        out_specs=[VMEM] * 11,
        scratch_shapes=[
            pltpu.VMEM((pairs, LANES), i32),
            pltpu.VMEM(atm_metric.shape, f32),
            pltpu.VMEM((pairs, LANES), i32),
            pltpu.VMEM((pairs, LANES), f32),
            pltpu.VMEM((pairs, LANES), i32),
            pltpu.VMEM((pairs, LANES), f32),
            pltpu.VMEM((pairs, LANES), i32),
            pltpu.VMEM((pairs, LANES), i32),
            pltpu.VMEM((pairs, LANES), f32),
            pltpu.VMEM((3, pairs, LANES), f32),
            pltpu.VMEM((pairs, LANES), f32),
            pltpu.VMEM((3 * pairs, 2 * LANES), jnp.bfloat16),
            pltpu.VMEM(made.shape, f32),
            pltpu.VMEM((3 * rows // LANES, LANES), f32),
            pltpu.VMEM((3 * rows // LANES, 2 * LANES), jnp.bfloat16),
            pltpu.VMEM(arriving.shape[1:], f32),
            pltpu.VMEM((3, levels, 2 * y_points), f32),
            pltpu.VMEM(((x_points + 2) * y_points + 16, LANES), f32),
            pltpu.VMEM((y_points + 16, LANES), f32),
            pltpu.VMEM((y_points + 16, LANES), f32),
            pltpu.SMEM((rows,), i32),
            pltpu.SMEM((y_points,), i32),
            pltpu.SMEM((y_points,), i32),
            pltpu.SMEM(wave_speed.shape, f32),
            dma((9,)),
            dma((n,)),
            dma((2, n)),
            dma((2,)),
            dma((2,)),
            dma((2,)),
            dma((2,)),
            dma,
            dma,
        ],
        compiler_params=pltpu.CompilerParams(collective_id=0, has_side_effects=True, **PARAMS),
        name="start",
    )(placed, slot_rows, source, weight, metric, adjacent, edges, speed)

    new_state, _ = pl.pallas_call(
        functools.partial(end_kernel, x_points, y_points),
        out_shape=[whole, table],
        in_specs=[VMEM] * 11 + [HBM] * 4,
        out_specs=[HBM, VMEM],
        input_output_aliases={6: 1},
        scratch_shapes=[
            pltpu.VMEM(state.shape, f32),
            pltpu.VMEM((pairs, LANES), f32),
            pltpu.VMEM((3, pairs, LANES), f32),
            pltpu.VMEM((3 * pairs, 2 * LANES), jnp.bfloat16),
            pltpu.VMEM((3, rows // LANES, LANES), f32),
            pltpu.VMEM((rows // LANES, LANES), f32),
            pltpu.VMEM(ocean_adjacent.shape, i32),
            pltpu.SMEM((rows,), i32),
            pltpu.SMEM((6, LANES), i32),
            pltpu.VMEM((rows + 2 * y_points, LANES), f32),
            pltpu.SMEM((y_points,), i32),
            pltpu.SMEM((y_points,), i32),
            pltpu.SMEM(couple_rate.shape, f32),
            dma((7,)),
            dma((4,)),
        ],
        compiler_params=pltpu.CompilerParams(**PARAMS),
        name="end",
    )(*held, kappa, adjacent, edges, rate)
    return new_state


def solution(mesh):
    in_specs = (
        P(None, None, ("sec", "dom")),
        P(("sec", "dom")),
        P(("sec", "dom")),
        P(("sec", "dom")),
        P("sec", None),
        P(None, "dom"),
        P(),
        P(None, "dom"),
        P(None, "dom"),
        P("dom"),
    )
    out_specs = P(None, None, ("sec", "dom"))
    return jax.shard_map(body, mesh=mesh, in_specs=in_specs, out_specs=out_specs, check_vma=False)
```

```python
import functools
import jax
import jax.numpy as jnp
import numpy as np
from jax import lax
from jax.experimental import pallas as pl
from jax.experimental.pallas import tpu as pltpu
from jax.sharding import PartitionSpec as P

TIME_STEP = 0.05
LANES = 128
VMEM = pl.BlockSpec(memory_space=pltpu.VMEM)
SMEM = pl.BlockSpec(memory_space=pltpu.SMEM)
HBM = pl.BlockSpec(memory_space=pltpu.HBM)
PARAMS = dict(vmem_limit_bytes=36 << 20)


def gll_derivative():
    nodes = np.array([-1.0, -1.0 / np.sqrt(5.0), 1.0 / np.sqrt(5.0), 1.0])
    barycentric = np.array(
        [1.0 / np.prod([nodes[i] - nodes[j] for j in range(4) if j != i]) for i in range(4)]
    )
    matrix = np.zeros((4, 4))
    for i in range(4):
        for j in range(4):
            if i != j:
                matrix[i, j] = barycentric[j] / barycentric[i] / (nodes[i] - nodes[j])
        matrix[i, i] = -np.sum(matrix[i])
    return matrix


DERIVATIVE = gll_derivative()


def lane_phase(shape):
    return lax.broadcasted_iota(jnp.int32, shape, 1) % 4


def along_second(value, phase):
    width = value.shape[1]
    total = jnp.zeros_like(value)
    for shift in range(-3, 4):
        factor = jnp.zeros(value.shape, jnp.float32)
        for i in range(4):
            if 0 <= i + shift < 4:
                factor = jnp.where(phase == i, np.float32(DERIVATIVE[i, i + shift]), factor)
        moved = value if shift == 0 else pltpu.roll(value, (-shift) % width, 1)
        total = total + factor * moved
    return total


def advance(x_points, y_points, state_ref, metric_ref, speed_ref, stepped_ref):
    level = lax.broadcasted_iota(jnp.int32, (state_ref.shape[1], LANES), 0)
    speed = jnp.zeros(level.shape, jnp.float32)
    for k in range(level.shape[0]):
        speed = jnp.where(level == k, speed_ref[k], speed)

    def piece(g, _):
        def at(i, f):
            return state_ref[f, :, pl.ds(pl.multiple_of(start + i * y_points, LANES), LANES)]

        start = (g // (y_points // LANES)) * 4 * y_points + (g % (y_points // LANES)) * LANES
        phase = lane_phase((state_ref.shape[1], LANES))
        u = [at(i, 0) for i in range(4)]
        v = [at(i, 1) for i in range(4)]
        h = [at(i, 2) for i in range(4)]
        for i in range(4):
            here = pl.ds(pl.multiple_of(start + i * y_points, LANES), LANES)
            gx = metric_ref[0:1, here]
            gy = metric_ref[1:2, here]
            dx_h = sum(np.float32(DERIVATIVE[i, j]) * h[j] for j in range(4))
            dx_u = sum(np.float32(DERIVATIVE[i, j]) * u[j] for j in range(4))
            stepped_ref[0, :, here] = u[i] - TIME_STEP * (gx * dx_h)
            stepped_ref[1, :, here] = v[i] - TIME_STEP * (gy * along_second(h[i], phase))
            spread = gx * dx_u + gy * along_second(v[i], phase)
            stepped_ref[2, :, here] = h[i] - TIME_STEP * speed * spread
        return 0

    lax.fori_loop(0, x_points // 4 * (y_points // LANES), piece, 0)


CHUNK = 32
KEEP = 32


def two_terms(table):
    high = table.astype(jnp.bfloat16)
    low = (table - high.astype(jnp.float32)).astype(jnp.bfloat16)
    return jnp.concatenate([high, low], axis=1)


def pick(terms, depth, low, high):
    count = low.shape[1]
    low = jnp.broadcast_to(low.astype(jnp.int16), (LANES, count))
    lane = lax.broadcasted_iota(jnp.int16, (LANES, LANES), 0)
    lane = jnp.concatenate([lane] * (count // LANES), axis=1)
    hot = jnp.where(lane == low, jnp.bfloat16(1), jnp.bfloat16(0))
    found = jnp.dot(terms, jnp.concatenate([hot, hot], axis=0), preferred_element_type=jnp.float32)
    high = jnp.broadcast_to(high, (8, count))
    own = lax.broadcasted_iota(jnp.int32, high.shape, 0) == (high & 7)
    picked = []
    for f in range(3):
        parts = [found[f * depth + 8 * i : f * depth + 8 * i + 8] for i in range(depth // 8)]
        bit = 3
        while len(parts) > 1:
            odd = ((high >> bit) & 1) == 1
            parts = [jnp.where(odd, parts[i + 1], parts[i]) for i in range(0, len(parts), 2)]
            bit += 1
        picked.append(jnp.sum(jnp.where(own, parts[0], 0.0), axis=0, keepdims=True))
    return picked


def row_of(ref, start, count):
    return jnp.concatenate([ref[pl.ds(start + r, 1), :] for r in range(count)], axis=1)


def split_pairs(source_ref, weight_ref, low_ref, high_ref, share_ref):
    i = lax.broadcasted_iota(jnp.int32, (LANES, LANES), 0)
    j = lax.broadcasted_iota(jnp.int32, (LANES, LANES), 1)
    half = LANES // 2
    chosen = (i == 2 * (j % half) + j // half).astype(jnp.float32).astype(jnp.bfloat16)

    def move(value):
        return jnp.dot(value.astype(jnp.bfloat16), chosen, preferred_element_type=jnp.float32)

    source = source_ref[...]
    low_ref[...] = (move((source & (LANES - 1)).astype(jnp.float32)) + 0.5).astype(jnp.int32)
    high_ref[...] = (move((source >> 7).astype(jnp.float32)) + 0.5).astype(jnp.int32)
    weight = weight_ref[...]
    upper = weight.astype(jnp.bfloat16).astype(jnp.float32)
    share_ref[...] = move(upper) + move(weight - upper)


def regrid_into(regrid_ref, arrived, low_ref, high_ref, share_ref, terms_ref, value_ref, ratio_ref):
    depth = low_ref.shape[0]
    for f in range(3):
        terms_ref[f * depth : (f + 1) * depth, :] = two_terms(arrived(f).reshape(depth, LANES))

    def step(c, _):
        low, high = row_of(low_ref, c * (2 * CHUNK), (2 * CHUNK)), row_of(high_ref, c * (2 * CHUNK), (2 * CHUNK))
        values = pick(terms_ref[...], depth, low, high)
        for f in range(3):
            for r in range((2 * CHUNK)):
                value_ref[f, pl.ds(c * (2 * CHUNK) + r, 1), :] = values[f][:, r * LANES : (r + 1) * LANES]
        return 0

    lax.fori_loop(0, depth // (2 * CHUNK), step, 0)
    share = share_ref[...]
    whole = share + pltpu.roll(share, LANES // 2, 1)
    first = lax.broadcasted_iota(jnp.int32, (depth // 2, LANES), 1) < LANES // 2
    for f in range(3):
        product = value_ref[f] * share
        ratio_ref[...] = (product + pltpu.roll(product, LANES // 2, 1)) / whole
        even = ratio_ref[pl.ds(0, depth // 2, stride=2), :]
        odd = ratio_ref[pl.ds(1, depth // 2, stride=2), :]
        regrid_ref[f] = jnp.where(first, even, odd)


def to_rows(source_ref, source_at, table_ref, table_at, count, name_at, unroll):
    def piece(c, _):
        here = pl.ds(pl.multiple_of(source_at + c * LANES, LANES), LANES)
        name = lax.broadcasted_iota(jnp.int32, (8, LANES), 1) + (name_at + c * LANES)
        kind = lax.broadcasted_iota(jnp.int32, (8, LANES), 0)
        name = jnp.where(kind < 6, name, jnp.where(kind == 6, 1, 0)).astype(jnp.float32)
        block = jnp.concatenate([source_ref[f, :, here] for f in range(3)] + [name], axis=0)
        there = pl.ds(pl.multiple_of(table_at + c * LANES, 8), LANES)
        table_ref[there, :KEEP] = jnp.transpose(block)
        return 0

    lax.fori_loop(0, count // LANES, piece, 0, unroll=unroll)


def walk(y_points, x_points, next_ref, first_ref, last_ref, visit, middle):
    def chain(c, _):
        base = pl.multiple_of(c * 8, 8)
        places = [first_ref[base + u] for u in range(8)]
        for x in range(x_points - 1):
            if x or not middle:
                visit(x, base, places)
            if x < x_points - 2:
                places = [next_ref[place] for place in places]
        if not middle:
            visit(x_points - 1, base, [last_ref[base + u] for u in range(8)])
        return 0

    lax.fori_loop(0, y_points // 8, chain, 0)


def start_kernel(
    n, x_points, y_points, state_hbm, rows_hbm, source_hbm, weight_hbm, metric_hbm, adjacent_hbm, edges_hbm, speed_hbm,
    state_ref, in_ref, regrid_ref, stepped_ref, west_ref, east_ref, table_ref, sum_ref, low_ref, high_ref, share_ref,
    rows_ref, metric_ref, source_ref, weight_ref, sea_source_ref, sea_weight_ref, sea_low_ref, sea_high_ref,
    sea_share_ref, value_ref, ratio_ref, pair_terms_ref, made_ref, surface_ref, terms_ref, out_ref, rim_ref, grid_ref,
    west_rim_ref, east_rim_ref, next_ref, first_ref, last_ref, speed_ref,
    load_sem, slot_send, slot_recv, edge_send, edge_recv, pair_send, pair_recv, made_send, made_recv,
):
    sec, dom = lax.axis_index("sec"), lax.axis_index("dom")
    right, left = lax.rem(dom + 1, n), lax.rem(dom + n - 1, n)
    mesh_ids = pl.DeviceIdType.MESH
    atmosphere, ocean = sec == 0, sec == 1
    load_state = pltpu.make_async_copy(state_hbm, state_ref, load_sem.at[0])
    load_rows = pltpu.make_async_copy(rows_hbm, rows_ref, load_sem.at[1])
    load_metric = pltpu.make_async_copy(metric_hbm, metric_ref, load_sem.at[2])
    load_next = pltpu.make_async_copy(adjacent_hbm.at[2], next_ref, load_sem.at[3])
    load_first = pltpu.make_async_copy(edges_hbm.at[0], first_ref, load_sem.at[4])
    load_last = pltpu.make_async_copy(edges_hbm.at[1], last_ref, load_sem.at[8])
    load_speed = pltpu.make_async_copy(speed_hbm, speed_ref, load_sem.at[5])
    load_source = pltpu.make_async_copy(source_hbm, source_ref, load_sem.at[6])
    load_weight = pltpu.make_async_copy(weight_hbm, weight_ref, load_sem.at[7])
    load_state.start()
    load_rows.start()
    barrier = pltpu.get_barrier_semaphore()

    def hello(a, b):
        pl.semaphore_signal(barrier, inc=1, device_id=(a, b), device_id_type=mesh_ids)

    @pl.when(atmosphere)
    def _():
        def greet(p, _):
            hello(1, p)

            @pl.when(p != dom)
            def _():
                hello(0, p)

            return 0

        lax.fori_loop(0, n, greet, 0)
        load_metric.start()
        load_speed.start()
        load_source.start()
        load_weight.start()

    @pl.when(ocean)
    def _():
        hello(0, dom)
        hello(1, left)
        hello(1, right)
        load_first.start()
        load_last.start()
        load_next.start()

    load_state.wait()
    depth, top, rows = state_ref.shape[2] // LANES, state_ref.shape[1] - 1, state_ref.shape[2]

    def visit(x, base, places):
        found = [table_ref[pl.ds(place, 1), :] for place in places]
        for u in range(len(places)):
            grid_ref[pl.ds(base + (8 + (x + 1) * y_points + u), 1), :] = found[u]

    @pl.when(ocean)
    def _():
        to_rows(state_ref, 0, table_ref, 0, rows, 0, 16)
        load_first.wait()
        load_last.wait()

        def edge(c, _):
            base = pl.multiple_of(c * 8, 8)
            for listed, x in ((first_ref, 0), (last_ref, x_points - 1)):
                visit(x, base, [listed[base + u] for u in range(8)])
            return 0

        lax.fori_loop(0, y_points // 8, edge, 0)
        levels = top + 1
        for k, x in ((0, 0), (1, x_points - 1)):
            for c in range(y_points // LANES):
                at = 8 + (x + 1) * y_points + c * LANES
                block = jnp.transpose(grid_ref[at : at + LANES, :KEEP])
                for f in range(3):
                    rim_ref[f, :, k * y_points + c * LANES : k * y_points + (c + 1) * LANES] = block[
                        f * levels : (f + 1) * levels
                    ]

    for f in range(3):
        for h in range(depth):
            surface_ref[f * depth + h : f * depth + h + 1, :] = state_ref[
                f, top : top + 1, h * LANES : (h + 1) * LANES
            ]
    terms_ref[...] = two_terms(surface_ref[...])
    load_rows.wait()

    def remote(source, target, send, recv, device):
        return pltpu.make_async_remote_copy(
            src_ref=source, dst_ref=target, send_sem=send, recv_sem=recv, device_id=device, device_id_type=mesh_ids
        )

    lines = out_ref.shape[2]
    peers = CHUNK // lines
    chunks = rows_ref.shape[0] // CHUNK

    def slots(p):
        return remote(out_ref.at[p], in_ref.at[sec, dom], slot_send.at[p], slot_recv.at[sec, dom], (0, p))

    def own_slots():
        return pltpu.make_async_copy(out_ref.at[dom], in_ref.at[0, dom], slot_recv.at[0, dom])

    pair_source = remote(source_hbm, sea_source_ref, pair_send.at[0], pair_recv.at[0], (0, dom))
    pair_weight = remote(weight_hbm, sea_weight_ref, pair_send.at[1], pair_recv.at[1], (0, dom))
    made = remote(made_ref, regrid_ref, made_send, made_recv, (1, dom))

    first, last = pl.ds(0, y_points), pl.ds(rows - y_points, y_points)
    rim_first, rim_last = rim_ref.at[:, :, first], rim_ref.at[:, :, pl.ds(y_points, y_points)]
    air_edges = [
        remote(stepped_ref.at[:, :, last], west_ref, edge_send.at[0], edge_recv.at[0], (0, right)),
        remote(stepped_ref.at[:, :, first], east_ref, edge_send.at[1], edge_recv.at[1], (0, left)),
    ]
    sea_edges = [
        remote(rim_last, west_ref, edge_send.at[0], edge_recv.at[0], (1, right)),
        remote(rim_first, east_ref, edge_send.at[1], edge_recv.at[1], (1, left)),
    ]

    def send(k, _):
        c = lax.rem(k + dom * chunks // n, chunks)
        index = row_of(rows_ref, c * CHUNK, CHUNK)
        values = pick(terms_ref[...], depth, index & (LANES - 1), index >> 7)
        for f in range(3):
            for r in range(CHUNK):
                out_ref[c * peers + r // lines, f, pl.ds(r % lines, 1), :] = values[f][:, r * LANES : (r + 1) * LANES]

        @pl.when(jnp.logical_and(k == 0, atmosphere))
        def _():
            pl.semaphore_wait(barrier, n)

        @pl.when(jnp.logical_and(k == 0, ocean))
        def _():
            pl.semaphore_wait(barrier, n + 2)
            for each in sea_edges:
                each.start()
            pair_source.start()
            pair_weight.start()

        def ship(j, _):
            p = c * peers + j
            here = jnp.logical_and(atmosphere, p == dom)

            @pl.when(here)
            def _():
                own_slots().start()

            @pl.when(jnp.logical_not(here))
            def _():
                slots(p).start()

            return 0

        lax.fori_loop(0, peers, ship, 0)
        return 0

    lax.fori_loop(0, chunks, send, 0)

    def sent(p, _):
        @pl.when(jnp.logical_not(jnp.logical_and(atmosphere, p == dom)))
        def _():
            slots(p).wait_send()

        return 0

    def arrival(a, p):
        remote(out_ref.at[p], in_ref.at[a, p], slot_send.at[p], slot_recv.at[a, p], (0, p)).wait_recv()

    @pl.when(atmosphere)
    def _():
        load_metric.wait()
        load_speed.wait()
        advance(x_points, y_points, state_ref, metric_ref, speed_ref, stepped_ref)
        for each in air_edges:
            each.start()
        load_source.wait()
        load_weight.wait()
        split_pairs(source_ref, weight_ref, low_ref, high_ref, share_ref)
        pair_source.wait_recv()
        pair_weight.wait_recv()
        split_pairs(sea_source_ref, sea_weight_ref, sea_low_ref, sea_high_ref, sea_share_ref)

        def from_air(p, _):
            @pl.when(p == dom)
            def _():
                own_slots().wait()

            @pl.when(p != dom)
            def _():
                arrival(0, p)

            return 0

        lax.fori_loop(0, n, from_air, 0)
        regrid_into(
            made_ref, lambda f: in_ref[0, :, f], sea_low_ref, sea_high_ref, sea_share_ref,
            pair_terms_ref, value_ref, ratio_ref,
        )
        made.start()

        def from_sea(p, _):
            arrival(1, p)
            return 0

        lax.fori_loop(0, n, from_sea, 0)
        for each in air_edges:
            each.wait()
        lax.fori_loop(0, n, sent, 0)
        made.wait_send()

    @pl.when(ocean)
    def _():
        load_next.wait()
        walk(y_points, x_points, next_ref, first_ref, last_ref, visit, True)
        rims = (west_rim_ref, east_rim_ref)
        sum_neighbours(x_points, y_points, grid_ref, rims, sum_ref, [range(1, x_points - 1)])
        for each in sea_edges:
            each.wait()
        to_rows(west_ref, 0, west_rim_ref, 8, y_points, rows, 4)
        to_rows(east_ref, 0, east_rim_ref, 8, y_points, rows + y_points, 4)
        sum_neighbours(x_points, y_points, grid_ref, rims, sum_ref, [range(1), range(x_points - 1, x_points)])
        pair_source.wait_send()
        pair_weight.wait_send()
        lax.fori_loop(0, n, sent, 0)
        made.wait_recv()


def sum_neighbours(x_points, y_points, grid_ref, rims, sum_ref, spans):
    lane = lax.broadcasted_iota(jnp.int32, (8, LANES), 1)
    row = lax.broadcasted_iota(jnp.int32, (8, LANES), 0)

    def mask(*names):
        kept = lane < 24
        for name in names:
            kept = kept | (lane == 24 + name)
        return kept.astype(jnp.float32)

    same, tilted = mask(2, 3), mask(4, 5)
    above, below = mask(0), mask(1)
    east, west = mask(2, 4), mask(3, 5)

    def read(x, at, shift):
        if 0 <= x < x_points:
            return grid_ref[pl.ds(at + (8 + (x + 1) * y_points + shift), 8), :]
        return rims[0 if x < 0 else 1][pl.ds(at + (8 + shift), 8), :]

    def inner(c, _):
        at = c * 8
        for span in spans:
            joined, upright = {}, {}
            for x in range(span.start - 1, span.stop + 1):
                middle, up, down = read(x, at, 0), read(x, at, 1), read(x, at, -1)
                joined[x] = middle * same + (down if x % 2 else up) * tilted
                upright[x] = up * above + down * below
                if x > span.start:
                    total = upright[x - 1] + joined[x] * east + joined[x - 2] * west
                    sum_ref[pl.ds(pl.multiple_of(at + (x - 1) * y_points, 8), 8), :] = total
        return 0

    lax.fori_loop(1, y_points // 8 - 1, inner, 0)

    for at, gone, missing in ((0, row == 0, -1), (y_points - 8, row == 7, 1)):
        for x in [x for span in spans for x in span]:
            own = read(x, at, 0)
            tilt = 1 if x % 2 else -1

            def near(x, shift):
                value = read(x, at, shift)
                return jnp.where(gone, own, value) if shift == missing else value

            total = near(x, 1) * above + near(x, -1) * below
            total = total + (near(x + 1, 0) * same + near(x + 1, tilt) * tilted) * east
            total = total + (near(x - 1, 0) * same + near(x - 1, tilt) * tilted) * west
            sum_ref[x * y_points + at : x * y_points + at + 8, :] = total


def end_kernel(
    x_points, y_points, state_ref, in_ref, made_ref, stepped_ref, west_ref, east_ref, table_in_ref, sum_ref,
    low_ref, high_ref, share_ref, kappa_hbm, adjacent_hbm, edges_hbm, rate_hbm,
    new_hbm, table_ref,
    new_ref, ratio_ref, value_ref, pair_terms_ref, regrid_ref, kappa_ref, adjacent_ref, next_ref, few_ref,
    every_ref, first_ref, last_ref, rate_ref, load_sem, store_sem,
):
    sec = lax.axis_index("sec")
    levels, rows = state_ref.shape[1], state_ref.shape[2]
    load_rate = pltpu.make_async_copy(rate_hbm, rate_ref, load_sem.at[0])
    load_next = pltpu.make_async_copy(adjacent_hbm.at[2], next_ref, load_sem.at[1])
    load_adjacent = pltpu.make_async_copy(adjacent_hbm, adjacent_ref, load_sem.at[2])
    load_kappa = pltpu.make_async_copy(kappa_hbm, kappa_ref, load_sem.at[3])
    load_first = pltpu.make_async_copy(edges_hbm.at[0], first_ref, load_sem.at[4])
    load_last = pltpu.make_async_copy(edges_hbm.at[1], last_ref, load_sem.at[6])
    load_rate.start()

    @pl.when(sec == 1)
    def _():
        load_first.start()
        load_last.start()
        load_next.start()
        load_adjacent.start()
        load_kappa.start()

    load_rate.wait()

    def couple(f, here, value, relaxed):
        row = lax.broadcasted_iota(jnp.int32, value.shape, 0)
        new_ref[f, :, here] = jnp.where(row == levels - 1, value + rate_ref[0, f] * (relaxed - value), value)

    @pl.when(sec == 0)
    def _():
        regrid_into(
            regrid_ref, lambda f: in_ref[1, :, f], low_ref, high_ref, share_ref, pair_terms_ref, value_ref, ratio_ref
        )
        stores = [pltpu.make_async_copy(new_ref.at[f], new_hbm.at[f], store_sem.at[f]) for f in range(3)]
        for f in range(3):
            for x in range(x_points):
                here = slice(x * y_points, (x + 1) * y_points)
                value = stepped_ref[f, :, here]
                if x % 4 == 3:
                    other = (
                        stepped_ref[f, :, (x + 1) * y_points : (x + 2) * y_points]
                        if x < x_points - 1
                        else east_ref[f]
                    )
                    value = (value + other) * 0.5
                elif x % 4 == 0:
                    other = stepped_ref[f, :, (x - 1) * y_points : x * y_points] if x else west_ref[f]
                    value = (value + other) * 0.5
                position = lax.broadcasted_iota(jnp.int32, value.shape, 1)
                phase = position % 4
                after = pltpu.roll(value, y_points - 1, 1)
                before = pltpu.roll(value, 1, 1)
                averaged = jnp.where(
                    (phase == 3) & (position < y_points - 1),
                    (value + after) * 0.5,
                    jnp.where((phase == 0) & (position > 0), (value + before) * 0.5, value),
                )
                lines = y_points // LANES
                relaxed = jnp.concatenate(
                    [regrid_ref[f, x * lines + i : x * lines + i + 1, :] for i in range(lines)], axis=1
                )
                couple(f, here, averaged, relaxed)
            stores[f].start()
        for each in stores:
            each.wait()

    @pl.when(sec == 1)
    def _():
        load_next.wait()
        load_first.wait()
        load_last.wait()

        def visit(x, base, places):
            found = [sum_ref[pl.ds(base + (x * y_points + u), 1), :] for u in range(len(places))]
            for u, place in enumerate(places):
                table_ref[pl.ds(place, 1), :] = found[u]

        walk(y_points, x_points, next_ref, first_ref, last_ref, visit, False)
        load_adjacent.wait()
        load_kappa.wait()
        part = rows // 4
        stores = [
            pltpu.make_async_copy(
                new_ref.at[:, :, pl.ds(k * part, part)], new_hbm.at[:, :, pl.ds(k * part, part)], store_sem.at[k]
            )
            for k in range(4)
        ]

        def finish(c, wrong):
            here = pl.ds(pl.multiple_of(c * LANES, LANES), LANES)
            block = jnp.transpose(table_ref[here, :KEEP])
            kappa = kappa_ref[pl.ds(c, 1), :]
            for f in range(3):
                value = state_ref[f, :, here]
                swept = value + kappa * (block[f * levels : (f + 1) * levels] - 6.0 * value)
                couple(f, here, swept, made_ref[f, pl.ds(c, 1), :])
            named = adjacent_ref[:, here].astype(jnp.float32)
            names = block[24:32]
            off = (names[0:6] != named).astype(jnp.float32)
            return jnp.maximum(wrong, jnp.maximum(jnp.max(off, axis=0, keepdims=True), names[6:7]))

        wrong = jnp.zeros((1, LANES), jnp.float32)
        for k in range(4):
            blocks = part // LANES
            wrong = lax.fori_loop(k * blocks, (k + 1) * blocks, finish, wrong, unroll=16)
            stores[k].start()
        for each in stores:
            each.wait()

        @pl.when(jnp.max(wrong) > 0.0)
        def _():
            to_rows(state_ref, 0, every_ref, 0, rows, 0, 1)
            to_rows(west_ref, 0, every_ref, rows, y_points, rows, 1)
            to_rows(east_ref, 0, every_ref, rows + y_points, y_points, rows + y_points, 1)

            def block(c, _):
                fetch = pltpu.make_async_copy(
                    adjacent_hbm.at[:, pl.ds(pl.multiple_of(c * LANES, LANES), LANES)], few_ref, load_sem.at[5]
                )
                fetch.start()
                fetch.wait()

                def cell(i, _):
                    total = every_ref[pl.ds(few_ref[0, i], 1), :]
                    for j in range(1, 6):
                        total = total + every_ref[pl.ds(few_ref[j, i], 1), :]
                    table_ref[pl.ds(c * LANES + i, 1), :] = total
                    return 0

                lax.fori_loop(0, LANES, cell, 0)
                return 0

            lax.fori_loop(0, rows // LANES, block, 0)
            lax.fori_loop(0, rows // LANES, finish, wrong)
            whole = pltpu.make_async_copy(new_ref, new_hbm, store_sem.at[0])
            whole.start()
            whole.wait()


def body(
    state, send_rows, intersection_source, intersection_weight, couple_rate, atm_metric, wave_speed,
    ocean_adjacent, ocean_edges, ocean_kappa,
):
    levels, rows = state.shape[1], state.shape[2]
    y_points = ocean_edges.shape[1]
    x_points = rows // y_points
    n = lax.axis_size("dom")
    slots = send_rows.shape[0]
    lines = slots // n // LANES
    f32, i32 = jnp.float32, jnp.int32
    pairs = slots // LANES
    source, weight = intersection_source.reshape(-1, LANES), intersection_weight.reshape(-1, LANES)
    placed, slot_rows, source, weight, metric, adjacent, kappa, edges, speed, rate = [
        pltpu.with_memory_space_constraint(each, pltpu.HBM)
        for each in (
            state, send_rows.reshape(-1, LANES), source, weight, atm_metric, ocean_adjacent,
            ocean_kappa.reshape(-1, LANES), ocean_edges, wave_speed, couple_rate,
        )
    ]

    border = jax.ShapeDtypeStruct((3, levels, y_points), f32)
    whole = jax.ShapeDtypeStruct(state.shape, f32)
    table = jax.ShapeDtypeStruct((rows, LANES), f32)
    index, share = jax.ShapeDtypeStruct((pairs, LANES), i32), jax.ShapeDtypeStruct((pairs, LANES), f32)
    arriving = jax.ShapeDtypeStruct((2, n, 3, lines, LANES), f32)
    made = jax.ShapeDtypeStruct((3, rows // LANES, LANES), f32)
    dma = pltpu.SemaphoreType.DMA
    held = pl.pallas_call(
        functools.partial(start_kernel, n, x_points, y_points),
        out_shape=[whole, arriving, made, whole, border, border, table, table, index, index, share],
        in_specs=[HBM] * 8,
        out_specs=[VMEM] * 11,
        scratch_shapes=[
            pltpu.VMEM((pairs, LANES), i32),
            pltpu.VMEM(atm_metric.shape, f32),
            pltpu.VMEM((pairs, LANES), i32),
            pltpu.VMEM((pairs, LANES), f32),
            pltpu.VMEM((pairs, LANES), i32),
            pltpu.VMEM((pairs, LANES), f32),
            pltpu.VMEM((pairs, LANES), i32),
            pltpu.VMEM((pairs, LANES), i32),
            pltpu.VMEM((pairs, LANES), f32),
            pltpu.VMEM((3, pairs, LANES), f32),
            pltpu.VMEM((pairs, LANES), f32),
            pltpu.VMEM((3 * pairs, 2 * LANES), jnp.bfloat16),
            pltpu.VMEM(made.shape, f32),
            pltpu.VMEM((3 * rows // LANES, LANES), f32),
            pltpu.VMEM((3 * rows // LANES, 2 * LANES), jnp.bfloat16),
            pltpu.VMEM(arriving.shape[1:], f32),
            pltpu.VMEM((3, levels, 2 * y_points), f32),
            pltpu.VMEM(((x_points + 2) * y_points + 16, LANES), f32),
            pltpu.VMEM((y_points + 16, LANES), f32),
            pltpu.VMEM((y_points + 16, LANES), f32),
            pltpu.SMEM((rows,), i32),
            pltpu.SMEM((y_points,), i32),
            pltpu.SMEM((y_points,), i32),
            pltpu.SMEM(wave_speed.shape, f32),
            dma((9,)),
            dma((n,)),
            dma((2, n)),
            dma((2,)),
            dma((2,)),
            dma((2,)),
            dma((2,)),
            dma,
            dma,
        ],
        compiler_params=pltpu.CompilerParams(collective_id=0, has_side_effects=True, **PARAMS),
        name="start",
    )(placed, slot_rows, source, weight, metric, adjacent, edges, speed)

    new_state, _ = pl.pallas_call(
        functools.partial(end_kernel, x_points, y_points),
        out_shape=[whole, table],
        in_specs=[VMEM] * 11 + [HBM] * 4,
        out_specs=[HBM, VMEM],
        input_output_aliases={6: 1},
        scratch_shapes=[
            pltpu.VMEM(state.shape, f32),
            pltpu.VMEM((pairs, LANES), f32),
            pltpu.VMEM((3, pairs, LANES), f32),
            pltpu.VMEM((3 * pairs, 2 * LANES), jnp.bfloat16),
            pltpu.VMEM((3, rows // LANES, LANES), f32),
            pltpu.VMEM((rows // LANES, LANES), f32),
            pltpu.VMEM(ocean_adjacent.shape, i32),
            pltpu.SMEM((rows,), i32),
            pltpu.SMEM((6, LANES), i32),
            pltpu.VMEM((rows + 2 * y_points, LANES), f32),
            pltpu.SMEM((y_points,), i32),
            pltpu.SMEM((y_points,), i32),
            pltpu.SMEM(couple_rate.shape, f32),
            dma((7,)),
            dma((4,)),
        ],
        compiler_params=pltpu.CompilerParams(**PARAMS),
        name="end",
    )(*held, kappa, adjacent, edges, rate)
    return new_state


def solution(mesh):
    in_specs = (
        P(None, None, ("sec", "dom")),
        P(("sec", "dom")),
        P(("sec", "dom")),
        P(("sec", "dom")),
        P("sec", None),
        P(None, "dom"),
        P(),
        P(None, "dom"),
        P(None, "dom"),
        P("dom"),
    )
    out_specs = P(None, None, ("sec", "dom"))
    return jax.shard_map(body, mesh=mesh, in_specs=in_specs, out_specs=out_specs, check_vma=False)
```
